32 devices in a mesh: dp: 8 (over z, y), fsdp: 4 (over x, core).
Axes of the slice: x: 2, y: 2, z: 4, core: 2. Of those that a mesh axis runs over, the one named last changes fastest.
Arguments:
- tokens: bfloat16 [8192, 1024], P(('dp', 'fsdp')), may hold values from -6 to 6
- offsets: int32 [8, 3], P('dp'), may hold values from 0 to 1023, as said below
- live_tokens: int32 [8192], P(('dp', 'fsdp')), may hold values from 0 to 1, as said below
- gain_mixer: bfloat16 [1024], P(('dp', 'fsdp')), may hold values from 0.099609375 to 1.8984375
- query_weight: bfloat16 [1024, 256], P(('dp', 'fsdp')), may hold values from -0.1875 to 0.1875
- key_weight: bfloat16 [1024, 256], P(('dp', 'fsdp')), may hold values from -0.1875 to 0.1875
- value_weight: bfloat16 [1024, 1024], P(('dp', 'fsdp')), may hold values from -0.1875 to 0.1875
- output_weight: bfloat16 [1024, 1024], P(('dp', 'fsdp')), may hold values from -1.5 to 1.5
- gain_feed: bfloat16 [1024], P(('dp', 'fsdp')), may hold values from 0.099609375 to 1.8984375
- gate_weight: bfloat16 [1024, 2752], P(('dp', 'fsdp')), may hold values from -0.1875 to 0.1875
- up_weight: bfloat16 [1024, 2752], P(('dp', 'fsdp')), may hold values from -0.1875 to 0.1875
- down_weight: bfloat16 [1024, 2752], P(('dp', 'fsdp')), may hold values from -0.109375 to 0.109375
- cotangent: bfloat16 [8192, 1024], P(('dp', 'fsdp')), may hold values from -6 to 6
Outputs:
- output: float32 [8192, 1024], P(('dp', 'fsdp'))
- tokens_grad: float32 [8192, 1024], P(('dp', 'fsdp'))
- gain_mixer_grad: float32 [1024], P(('dp', 'fsdp'))
- query_weight_grad: float32 [1024, 256], P(('dp', 'fsdp'))
- key_weight_grad: float32 [1024, 256], P(('dp', 'fsdp'))
- value_weight_grad: float32 [1024, 1024], P(('dp', 'fsdp'))
- output_weight_grad: float32 [1024, 1024], P(('dp', 'fsdp'))
- gain_feed_grad: float32 [1024], P(('dp', 'fsdp'))
- gate_weight_grad: float32 [1024, 2752], P(('dp', 'fsdp'))
- up_weight_grad: float32 [1024, 2752], P(('dp', 'fsdp'))
- down_weight_grad: float32 [1024, 2752], P(('dp', 'fsdp'))
The draws below stay inside these ranges and needn't reach their ends.
Inputs may be any that keep to these rules, and one draw needn't show every extreme that they name: `offsets`: each row rises strictly from 0; the second document of every group starts at or after position 128 and before position 256 of the stream, and ends within its last 256 positions; in one group the last document is a single token at the stream's last position. `live_tokens`: padding lies only at the ends of documents; every document begins with a real token, and the second document of every group ends in padding.
All inputs are finite; a program needn't handle non-finite values.
Results may differ from the reference program's by a relative error of at most 0.014.
Values may be sent and summed in bfloat16 or wider, within the bound.
No kernel may reach another device: no remote copies, remote signals or barrier semaphores. Data moves between devices by JAX's collectives and lax.ppermute only.
A program may use at most 120 MiB of HBM per device.

```python
import jax
import jax.numpy as jnp
from jax import lax

D = 1024
HEADS = 16
FDIM = 16
VDIM = 64
FF = 2752
FEAT = 273
TOK_DEV = 256
BLOCK = 256
GROUP = 1024
TOKENS = 8192
N_DP = 8
N_FSDP = 4


def packing(key):
    key_second, key_end, key_row = jax.random.split(key, 3)
    stream = TOK_DEV * N_FSDP
    second = jax.random.randint(key_second, (N_DP, 1), TOK_DEV // 2, TOK_DEV)
    spanned_end = jax.random.randint(key_end, (N_DP, 1), (N_FSDP - 1) * TOK_DEV + 1, stream)
    lucky = jax.random.randint(key_row, (), 0, N_DP)
    last_column = jnp.where(jnp.arange(N_DP, dtype=jnp.int32)[:, None] == lucky, stream - 1, spanned_end)
    return jnp.concatenate([jnp.zeros((N_DP, 1), jnp.int32), second, last_column], axis=1).astype(jnp.int32)


def draw_offsets(key, part):
    shared = packing(key)
    return shared


def draw_live_tokens(key, part):
    bounds = packing(key)
    key = jax.random.fold_in(key, 7)
    stream = TOK_DEV * N_FSDP
    ends = jnp.concatenate([bounds[:, 1:], jnp.full((N_DP, 1), stream, jnp.int32)], axis=1)
    lengths = ends - bounds
    floor_pad = jnp.zeros_like(lengths).at[:, 1].set(1)
    padding = jax.random.randint(key, lengths.shape, floor_pad, lengths // 4 + 1)
    places = jnp.arange(stream, dtype=jnp.int32)[None, :, None]
    inside = (places >= bounds[:, None, :]) & (places < (ends - padding)[:, None, :])
    return jnp.any(inside, axis=2).astype(jnp.int32).reshape(TOKENS)


def raised(values, key, source, target, blocks, factor):
    def block_of(dim):
        return (jnp.arange(values.shape[dim]) // (values.shape[dim] // blocks)).reshape((-1,) + (1,) * (values.ndim - 1 - dim))

    near = jax.random.permutation(key, blocks)[block_of(target)]
    second = (block_of(target) + blocks // 2) % blocks
    return jnp.where((block_of(source) == near) | (block_of(source) == second), factor * values, values)


def level_of(rng, dims, pieces, least, top_value):
    level, own = 1.0, jax.random.fold_in(rng, 6)
    for position, blocks in pieces:
        steps = jnp.exp(jax.random.uniform(jax.random.fold_in(own, position), (blocks,), jnp.float32, least / len(pieces), top_value / len(pieces)))
        level = level * jnp.repeat(steps, dims[position] // blocks).reshape([-1 if axis == position else 1 for axis in range(len(dims))])
    return level


def normal_values(rng, shape, scale, limit, cuts=(), kind=jnp.bfloat16):
    values = scale * jax.random.normal(rng, shape, jnp.float32)
    if cuts:
        values = values * level_of(rng, shape, cuts, -0.22, 0.18)
    return jnp.clip(values, -limit, limit).astype(kind)


def heavy_noise(own_key, dims, scale, limit, shards, heavy, held_as=jnp.bfloat16):
    array = scale * jax.random.normal(own_key, dims, jnp.float32)
    if shards:
        array = array * level_of(own_key, dims, shards, -0.22, 0.18)
    return jnp.clip(raised(array, jax.random.fold_in(own_key, 3), *heavy), -limit, limit).astype(held_as)


def setup_inputs(seed: int = 0) -> dict:
    splits = jax.random.split(jax.random.key(seed), 14)
    return {
        "tokens": heavy_noise(splits[0], (TOKENS, D), 1.0, 6.0, ((0, 32),), (0, 1, 32, 2.75)),
        "offsets": draw_offsets(jax.random.fold_in(splits[13], 71), 0),
        "live_tokens": draw_live_tokens(jax.random.fold_in(splits[13], 71), 0),
        "gain_mixer": jnp.clip(1.0 + 0.18 * jax.random.normal(splits[3], (D,), jnp.float32), 0.099609375, 1.8984375).astype(jnp.bfloat16),
        "query_weight": normal_values(splits[4], (D, HEADS * FDIM), D ** -0.5, 0.1875, ((0, 32),)),
        "key_weight": normal_values(splits[5], (D, HEADS * FDIM), D ** -0.5, 0.1875, ((0, 32),)),
        "value_weight": normal_values(splits[6], (D, HEADS * VDIM), D ** -0.5, 0.1875, ((0, 32),)),
        "output_weight": normal_values(splits[7], (HEADS * VDIM, D), (D // 64) ** -0.5, 1.5, ((0, 32),)),
        "gain_feed": jnp.clip(1.0 + 0.18 * jax.random.normal(splits[8], (D,), jnp.float32), 0.099609375, 1.8984375).astype(jnp.bfloat16),
        "gate_weight": normal_values(splits[9], (D, FF), D ** -0.5, 0.1875, ((0, 32),)),
        "up_weight": normal_values(splits[10], (D, FF), D ** -0.5, 0.1875, ((0, 32),)),
        "down_weight": normal_values(splits[11], (D, FF), FF ** -0.5, 0.109375, ((0, 32),)),
        "cotangent": heavy_noise(splits[12], (TOKENS, D), 1.0, 6.0, ((0, 32),), (0, 1, 32, 2.75)),
    }


@jax.custom_vjp
def low(v):
    return lax.optimization_barrier(v.astype(jnp.bfloat16)).astype(jnp.float32)

@jax.custom_vjp
def low_back(v):
    return v

def low_keep(v):
    return (low(v), None)

def low_pass(kept, grad):
    return (grad,)

def back_keep(v):
    return (v, None)

def back_low(kept, grad):
    return (low(grad),)
low.defvjp(low_keep, low_pass)
low_back.defvjp(back_keep, back_low)
epsilon = 1e-05
quad_scale = 0.25 * 0.7071067811865476

def normed(values, gain):
    return values * lax.rsqrt(lax.optimization_barrier(jnp.mean(values * values, axis=-1, keepdims=True)) + epsilon) * gain

def taylor(values):
    linear = values * 0.5
    square = values[..., :, None] * values[..., None, :] * quad_scale
    square = square.reshape(values.shape[:-1] + (values.shape[-1] * values.shape[-1],))
    constant = jnp.ones(values.shape[:-1] + (1,), jnp.float32)
    return jnp.concatenate([constant, linear, square], axis=-1)

def block_step(carry, items):
    state_in, sums_in = carry
    query_feat, key_feat, value_rows, doc_start, first_row = items
    places = jnp.arange(BLOCK, dtype=jnp.int32)
    allowed = ((doc_start[:, None] == doc_start[None, :]) & (places[None, :] <= places[:, None])).astype(jnp.float32)
    scores = jnp.einsum('thf,jhf->htj', query_feat, key_feat, precision=lax.Precision.HIGHEST)
    kept = low_back(scores * allowed[None])
    weights = low(kept)
    carried = (doc_start < first_row).astype(jnp.float32)
    denominator = lax.optimization_barrier(jnp.sum(kept, axis=-1)).T + carried[:, None] * jnp.einsum('thf,hf->th', query_feat, sums_in, precision=lax.Precision.HIGHEST)
    numerator = jnp.einsum('htj,jhe->the', weights, value_rows, precision=lax.Precision.HIGHEST)
    numerator = numerator + carried[:, None, None] * jnp.einsum('thf,hfe->the', query_feat, low(state_in), precision=lax.Precision.HIGHEST)
    numerator = low_back(numerator)
    mixed = low(numerator / denominator[:, :, None])
    chosen = (doc_start == doc_start[-1]).astype(jnp.float32)
    restart = (doc_start[-1] >= first_row).astype(jnp.float32)
    increment = low_back(jnp.einsum('jhf,jhe->hfe', key_feat * chosen[:, None, None], value_rows, precision=lax.Precision.HIGHEST))
    key_added = jnp.einsum('jhf,j->hf', key_feat, chosen, precision=lax.Precision.HIGHEST)
    state_out = (1.0 - restart) * state_in + increment
    sums_out = (1.0 - restart) * sums_in + key_added
    return ((state_out, sums_out), mixed)

def attend(query_feat, key_feat, value_rows, doc_start):
    length = query_feat.shape[0]
    count = length // BLOCK
    firsts = jnp.arange(count, dtype=jnp.int32) * BLOCK
    items = (query_feat.reshape(count, BLOCK, HEADS, FEAT), key_feat.reshape(count, BLOCK, HEADS, FEAT), value_rows.reshape(count, BLOCK, HEADS, VDIM), doc_start.reshape(count, BLOCK), firsts)
    start_state = (jnp.zeros((HEADS, FEAT, VDIM), jnp.float32), jnp.zeros((HEADS, FEAT), jnp.float32))
    unused, outputs = lax.scan(jax.checkpoint(block_step), start_state, items)
    return outputs.reshape(length, HEADS * VDIM)

def layer(inputs, doc_start, keep, gain_mixer, query_weight, key_weight, value_weight, output_weight, gain_feed, gate_weight, up_weight, down_weight):
    length = inputs.shape[0]
    hidden_one = low(normed(inputs, gain_mixer))
    query_raw = low_back(jnp.dot(hidden_one, query_weight, precision=lax.Precision.HIGHEST))
    key_raw = low_back(jnp.dot(hidden_one, key_weight, precision=lax.Precision.HIGHEST))
    value_rows = low(low_back(jnp.dot(hidden_one, value_weight, precision=lax.Precision.HIGHEST)))
    query_feat = low(taylor(query_raw.reshape(length, HEADS, FDIM)))
    key_feat = low(taylor(key_raw.reshape(length, HEADS, FDIM)) * keep[:, None, None])
    mixed = attend(query_feat, key_feat, value_rows.reshape(length, HEADS, VDIM), doc_start)
    after = inputs + low_back(jnp.dot(mixed, output_weight, precision=lax.Precision.HIGHEST))
    hidden_two = low(normed(after, gain_feed))
    gate_raw = low_back(jnp.dot(hidden_two, gate_weight, precision=lax.Precision.HIGHEST))
    lift_raw = low_back(jnp.dot(hidden_two, up_weight, precision=lax.Precision.HIGHEST))
    inner_act = low(jax.nn.silu(gate_raw) * lift_raw)
    return after + low_back(jnp.dot(inner_act, down_weight.T, precision=lax.Precision.HIGHEST))

def reference(tokens, offsets, live_tokens, gain_mixer, query_weight, key_weight, value_weight, output_weight, gain_feed, gate_weight, up_weight, down_weight, cotangent):
    params = (gain_mixer.astype(jnp.float32), query_weight.astype(jnp.float32), key_weight.astype(jnp.float32), value_weight.astype(jnp.float32), output_weight.astype(jnp.float32), gain_feed.astype(jnp.float32), gate_weight.astype(jnp.float32), up_weight.astype(jnp.float32), down_weight.astype(jnp.float32))
    places = jnp.arange(GROUP, dtype=jnp.int32)
    doc_starts = lax.optimization_barrier(jnp.max(jnp.where(offsets[:, None, :] <= places[None, :, None], offsets[:, None, :], 0), axis=2)).astype(jnp.int32)
    inputs = tokens.astype(jnp.float32).reshape(N_DP, GROUP, D)
    keep = live_tokens.astype(jnp.float32).reshape(N_DP, GROUP)
    incoming = cotangent.astype(jnp.float32).reshape(N_DP, GROUP, D)

    def one_group(running, items):
        group_in, group_start, group_keep, group_grad = items

        def forward(values, *weights):
            return layer(values, group_start, group_keep, *weights)
        result, pullback = jax.vjp(forward, group_in, *params)
        gradients = pullback(group_grad)
        running = tuple((total_now + added_now for total_now, added_now in zip(running, gradients[1:])))
        return (running, (result, gradients[0]))
    zeros_start = tuple((jnp.zeros(weight_now.shape, jnp.float32) for weight_now in params))
    totals, (results, input_grads) = lax.scan(one_group, zeros_start, (inputs, doc_starts, keep, incoming))
    return (results.reshape(TOKENS, D), input_grads.reshape(TOKENS, D), totals[0], totals[1], totals[2], totals[3], totals[4], totals[5], totals[6], totals[7], totals[8])
```

```python
import functools

import jax
import jax.numpy as jnp
from jax import lax
from jax.experimental import pallas as pl
from jax.experimental.pallas import tpu as pltpu
from jax.sharding import PartitionSpec as P

HEADS = 16
FDIM = 16
VDIM = 64
EPS = 1e-05

F32 = jnp.float32
BF16 = jnp.bfloat16
TILE = 256


def dot(a, b, dims=((1,), (0,))):
    return lax.dot_general(a, b, (dims, ((), ())), preferred_element_type=F32)


NT = ((1,), (1,))
TN = ((0,), (0,))


def swap(a, axis, bit):
    n = lax.axis_size(axis)
    return lax.ppermute(a, axis, [(i, i ^ bit) for i in range(n)])


def put_kernel(moves, axis, step, at_ref, *refs):
    sources, out = refs[:-1], refs[-1]
    for number, (source, first, size) in enumerate(moves):
        where = pl.ds(pl.multiple_of(at_ref[number], step), size)
        if axis == 0:
            out[where, :] = sources[source][first : first + size, :]
        else:
            out[:, where] = sources[source][...]


def put(pieces, moves, starts, axis, step, shape):
    return pl.pallas_call(
        functools.partial(put_kernel, moves, axis, step),
        out_shape=jax.ShapeDtypeStruct(shape, pieces[0].dtype),
        in_specs=[pl.BlockSpec(memory_space=pltpu.SMEM)] + [pl.BlockSpec(memory_space=pltpu.VMEM)] * len(pieces),
        out_specs=pl.BlockSpec(memory_space=pltpu.VMEM),
        compiler_params=pltpu.CompilerParams(vmem_limit_bytes=LIMIT),
    )(jnp.stack(starts).astype(jnp.int32), *pieces)


def pick(flag, one, two):
    return jnp.where(flag == 0, jnp.concatenate([one, two], 0), jnp.concatenate([two, one], 0))


def part(a, start, size):
    return lax.dynamic_slice_in_dim(a, start, size, 0)


def team_pieces(a):
    far = swap(a, "fsdp", 2)
    return a, swap(a, "fsdp", 1), far, swap(far, "fsdp", 1)


def team_gather(a, place, axis):
    size = a.shape[axis]
    shape = list(a.shape)
    shape[axis] *= 4
    starts = [(place ^ k) * size for k in range(4)]
    moves = tuple((k, 0, size) for k in range(4))
    return put(team_pieces(a), moves, starts, axis, size, tuple(shape))


def team_exchange(a, place):
    high, low = place // 2, place % 2
    rows = a.shape[0] // 4
    block = lambda j: part(a, j * rows, rows)
    give = jnp.concatenate([block(place ^ 1), block(place ^ 3)], 0)
    got = swap(give, "fsdp", 1)
    near = pick(low, block(place), got[:rows])
    away = pick(low, block(place ^ 2), got[rows:])
    return pick(high, near, swap(away, "fsdp", 2))


def team_exchange_late(a, place):
    rows = a.shape[0] // 4
    half = 2 * rows
    high, low = place // 2, place % 2
    mine = part(a, high * half, half)
    far = swap(part(a, (1 - high) * half, half), "fsdp", 2)
    give = jnp.concatenate([part(mine, (1 - low) * rows, rows), part(far, (1 - low) * rows, rows)], 0)
    got = swap(give, "fsdp", 1)
    return part(mine, low * rows, rows), got[:rows], part(far, low * rows, rows), got[rows:]


def team_sum(a, place):
    high = place // 2
    rows = a.shape[0] // 4
    block = lambda j: part(a, j * rows, rows)
    near = block(place ^ 1), block(place ^ 3)
    got = swap(jnp.concatenate(near, 0).astype(BF16), "fsdp", 1).astype(F32)
    keep = block(place).astype(F32) + got[:rows]
    give = block(place ^ 2).astype(F32) + got[rows:]
    return keep + swap(give.astype(BF16), "fsdp", 2).astype(F32)


def gather_rows(a):
    n = lax.axis_size("dp")
    if n != 8:
        return lax.all_gather(a, "dp", axis=0, tiled=True)
    at = lax.axis_index("dp")
    z, y = at // 2, at % 2
    rows = a.shape[0]
    mine = jnp.concatenate([a] + [swap(a, "dp", 2 * k) for k in (1, 2, 3)], 0)
    other = swap(mine, "dp", 1)
    moves = tuple((source, k * rows, rows) for source in range(2) for k in range(4))
    starts = [(2 * (z ^ k) + (y ^ source)) * rows for source in range(2) for k in range(4)]
    return put([mine, other], moves, starts, 0, rows, (8 * rows, a.shape[1]))


def scatter_rows(left, right):
    n = lax.axis_size("dp")
    if n != 8:
        return lax.psum_scatter(dot(left, right, TN), "dp", scatter_dimension=0, tiled=True)
    at = lax.axis_index("dp")
    z, y = at // 2, at % 2
    rows = left.shape[1] // 8
    half = lambda bit: jnp.concatenate(
        [lax.dynamic_slice_in_dim(left, (2 * k + bit) * rows, rows, 1) for k in range(4)], axis=1
    )
    give = dot(half(1 - y), right, TN).astype(BF16)
    keep = dot(half(y), right, TN)
    a = keep + swap(give, "dp", 1).astype(F32)
    total = part(a, z * rows, rows)
    for k in (1, 2, 3):
        total = total + swap(part(a, (z ^ k) * rows, rows).astype(BF16), "dp", 2 * k).astype(F32)
    return total


def lane_of(shape):
    return lax.broadcasted_iota(jnp.int32, shape, len(shape) - 1)


def query_cols(both):
    high = both.astype(BF16).astype(F32)
    low = both - high
    left = lane_of(both.shape) < 64
    one = jnp.where(left, high, pltpu.roll(low, 64, 1))
    two = jnp.where(left, high, 0.0)
    return jnp.concatenate([one.astype(BF16), two.astype(BF16)], axis=1)


def key_cols(both):
    high = both.astype(BF16).astype(F32)
    low = both - high
    left = lane_of(both.shape) < 64
    one = jnp.where(left, pltpu.roll(high, 64, 1), high)
    two = jnp.where(left, pltpu.roll(low, 64, 1), 0.0)
    return jnp.concatenate([one.astype(BF16), two.astype(BF16)], axis=1)


def head_only(a, h, width):
    lane = lane_of(a.shape)
    if width == FDIM:
        lane = lane % 64
    return jnp.where(lane // width == h, a, jnp.zeros_like(a))


def allowed(start, row, i, j):
    ok = row >= start
    if i == j:
        place = i * TILE + lax.broadcasted_iota(jnp.int32, (TILE, TILE), 0)
        ok = ok & (row <= place)
    return ok


def forward_kernel(x_ref, w_ref, start_ref, row_ref, raw_ref, mixed_ref, exact_ref, den_ref, qc, kc, vc):
    blocks = x_ref.shape[0] // TILE
    team_heads = vc.shape[1] // VDIM
    for i in range(blocks):
        at = pl.ds(i * TILE, TILE)
        x = x_ref[at, :]
        wide = x.astype(F32)
        scale = lax.rsqrt(jnp.mean(wide * wide, axis=1, keepdims=True) + EPS)
        raw = dot(x, w_ref[...]) * scale
        raw_ref[at, :] = raw
        both = raw[:, :128]
        qc[at, :] = query_cols(both)
        kc[at, :] = key_cols(both)
        vc[at, :] = raw[:, 128:].astype(BF16)
    for i in range(blocks):
        at = pl.ds(i * TILE, TILE)
        start = start_ref[at, :]
        q = qc[at, :]
        result = jnp.zeros((TILE, vc.shape[1]), F32)
        dens = jnp.zeros((TILE, 128), F32)
        for h in range(team_heads):
            total = jnp.zeros((TILE, vc.shape[1]), F32)
            den = jnp.zeros((TILE, 1), F32)
            for j in range(i + 1):
                there = pl.ds(j * TILE, TILE)
                s = dot(q, head_only(kc[there, :], h, FDIM), NT)
                kept = 1.0 + s * (0.25 + s * 0.03125)
                kept = jnp.where(allowed(start, row_ref[:, there], i, j), kept, 0.0)
                den = den + jnp.sum(kept, axis=1, keepdims=True)
                total = total + dot(kept.astype(BF16), vc[there, :])
            result = jnp.where(lane_of(result.shape) // VDIM == h, total / den, result)
            dens = jnp.where(lane_of(dens.shape) == h, den, dens)
        exact_ref[at, :] = result
        mixed_ref[at, :] = result.astype(BF16)
        den_ref[at, :] = dens


def backward_kernel(raw_ref, grad_ref, wo_ref, exact_ref, den_ref, start_ref, row_ref, scale_ref, back_ref, qc, kc, qr, kr, vc, acc):
    blocks = raw_ref.shape[0] // TILE
    team_heads = vc.shape[1] // VDIM
    for i in range(blocks):
        at = pl.ds(i * TILE, TILE)
        raw = raw_ref[at, :]
        both = raw[:, :128]
        qc[at, :] = query_cols(both)
        kc[at, :] = key_cols(both)
        turned = pltpu.roll(both, 64, 1)
        left = lane_of(both.shape) < 64
        kr[at, :] = jnp.where(left, turned, 0.0).astype(BF16)
        qr[at, :] = jnp.where(left, 0.0, turned).astype(BF16)
        vc[at, :] = raw[:, 128:].astype(BF16)
    acc[...] = jnp.zeros_like(acc)
    for i in range(blocks):
        at = pl.ds(i * TILE, TILE)
        start = start_ref[at, :]
        q = qc[at, :]
        grad = dot(grad_ref[at, :], wo_ref[...], NT)
        product = grad * exact_ref[at, :]
        dens = den_ref[at, :]
        for h in range(team_heads):
            inverse = 1.0 / jnp.sum(jnp.where(lane_of(dens.shape) == h, dens, 0.0), axis=1, keepdims=True)
            numer = head_only(grad * inverse, h, VDIM).astype(BF16)
            denom = -jnp.sum(head_only(product, h, VDIM), axis=1, keepdims=True) * inverse
            mine = head_only(qr[at, :], h, FDIM)
            back = jnp.zeros((TILE, 128), F32)
            for j in range(i + 1):
                there = pl.ds(j * TILE, TILE)
                s = dot(q, head_only(kc[there, :], h, FDIM), NT)
                ok = allowed(start, row_ref[:, there], i, j)
                kept = jnp.where(ok, 1.0 + s * (0.25 + s * 0.03125), 0.0)
                inner = dot(numer, vc[there, :], NT) + denom
                inner = jnp.where(ok, inner * (0.25 + s * 0.0625), 0.0).astype(BF16)
                back = back + dot(inner, head_only(kr[there, :], h, FDIM))
                acc[there, :128] += dot(inner, mine, TN)
                acc[there, 128:] += dot(kept.astype(BF16), numer, TN)
            acc[at, :128] += back
    for i in range(blocks):
        at = pl.ds(i * TILE, TILE)
        back_ref[at, :] = (acc[at, :] * scale_ref[at, :]).astype(BF16)


LIMIT = 60 * 1024 * 1024


def attend(x, w, start, row):
    length, width = x.shape[0], w.shape[1]
    value = width - 128
    return pl.pallas_call(
        forward_kernel,
        out_shape=(
            jax.ShapeDtypeStruct((length, width), F32),
            jax.ShapeDtypeStruct((length, value), BF16),
            jax.ShapeDtypeStruct((length, value), F32),
            jax.ShapeDtypeStruct((length, 128), F32),
        ),
        scratch_shapes=[
            pltpu.VMEM((length, 256), BF16),
            pltpu.VMEM((length, 256), BF16),
            pltpu.VMEM((length, value), BF16),
        ],
        compiler_params=pltpu.CompilerParams(vmem_limit_bytes=LIMIT),
    )(x, w, start, row)


def attend_back(raw, grad, wo, exact, den, start, row, scale):
    length, width = raw.shape
    value = width - 128
    return pl.pallas_call(
        backward_kernel,
        out_shape=jax.ShapeDtypeStruct((length, width), BF16),
        scratch_shapes=[
            pltpu.VMEM((length, 256), BF16),
            pltpu.VMEM((length, 256), BF16),
            pltpu.VMEM((length, 128), BF16),
            pltpu.VMEM((length, 128), BF16),
            pltpu.VMEM((length, value), BF16),
            pltpu.VMEM((length, width), F32),
        ],
        compiler_params=pltpu.CompilerParams(vmem_limit_bytes=LIMIT),
    )(raw, grad, wo, exact, den, start, row, scale)


def quarters(w, team):
    size = w.shape[1] // team
    return [w[:, k * size : (k + 1) * size] for k in range(team)]


def body(
    tokens,
    offsets,
    live_tokens,
    gain_mixer,
    query_weight,
    key_weight,
    value_weight,
    output_weight,
    gain_feed,
    gate_weight,
    up_weight,
    down_weight,
    cotangent,
):
    team = lax.axis_size("fsdp")
    place = lax.axis_index("fsdp")
    height, model = tokens.shape
    own_rows = gain_mixer.shape[0]
    length = height * team
    units = gate_weight.shape[1] // team
    kq, kv, ko = query_weight.shape[1] // team, value_weight.shape[1] // team, output_weight.shape[1] // team

    mixer_col = gain_mixer.astype(F32)[:, None]
    feed_col = gain_feed.astype(F32)[:, None]
    scaled = lambda w, g: (w.astype(F32) * g).astype(BF16)

    def stacked(*weights):
        cut = [quarters(w, team) for w in weights]
        return jnp.concatenate([jnp.concatenate([w[k] for w in cut], axis=1) for k in range(team)], axis=0)

    first = stacked(
        scaled(query_weight, mixer_col),
        scaled(key_weight, mixer_col),
        scaled(value_weight, mixer_col),
        output_weight,
    )
    first = gather_rows(team_exchange(first, place))
    live_row = jnp.pad(live_tokens.astype(BF16)[None, :], ((0, 15), (0, model - height)))
    packed = team_gather(jnp.concatenate([tokens, live_row], axis=0), place, 0).reshape(team, height + 16, model)
    x = packed[:, :height].reshape(length, model)
    live = packed[:, height, :height].reshape(length)

    feed = team_exchange(stacked(scaled(gate_weight, feed_col), scaled(up_weight, feed_col), down_weight), place)
    gate_up = gather_rows(feed[:, : 2 * units])
    down = gather_rows(feed[:, 2 * units :])
    w_qkv = first[:, : 2 * kq + kv]
    w_out = team_gather(first[:, 2 * kq + kv :], place, 1)
    cot = team_gather(cotangent, place, 0)

    positions = jnp.arange(length, dtype=jnp.int32)
    bounds = offsets[0]
    start = jnp.max(jnp.where(bounds[None, :] <= positions[:, None], bounds[None, :], 0), axis=1)
    start_col = start[:, None]
    key_row = jnp.where(live > 0, positions, -1)[None, :]

    raw, mixed, exact, den = attend(x, w_qkv, start_col, key_row)
    mixed = team_gather(mixed, place, 1)
    after = x.astype(F32) + dot(mixed, w_out)
    scale_two = lax.rsqrt(jnp.mean(after * after, axis=1, keepdims=True) + EPS)
    hidden = (after * scale_two).astype(BF16)
    both = dot(hidden, gate_up)
    gate, lift = both[:, :units], both[:, units:]
    sig = jax.nn.sigmoid(gate)
    act = (gate * sig * lift).astype(BF16)
    own = lambda a: lax.dynamic_slice_in_dim(a, place * height, height, 0)
    after_own, scale_own = own(after), own(scale_two)
    output = after_own + team_sum(dot(act, down, NT), place)

    grad_act = dot(cot, down)
    gate_back = (grad_act * lift * sig * (1.0 + gate * (1.0 - sig))).astype(BF16)
    lift_back = (grad_act * gate * sig).astype(BF16)
    back = jnp.concatenate([gate_back, lift_back], axis=1)
    grad_hidden = team_sum(dot(back, gate_up, NT), place)
    down_part = scatter_rows(cot, act)
    feed_part = scatter_rows(hidden, back)
    inner = jnp.mean(after_own * grad_hidden, axis=1, keepdims=True)
    grad_after = cotangent.astype(F32) + scale_own * grad_hidden - after_own * (scale_own * scale_own * scale_own * inner)
    grad_attn = team_gather(grad_after.astype(BF16), place, 0)

    wo_own = lax.dynamic_slice_in_dim(w_out, place * kv, kv, 0)
    out_part = scatter_rows(mixed, lax.dynamic_slice_in_dim(grad_attn, place * ko, ko, 1))
    wide = x.astype(F32)
    scale_one = lax.rsqrt(jnp.mean(wide * wide, axis=1, keepdims=True) + EPS)
    qkv_back = attend_back(raw, grad_attn, wo_own, exact, den, start_col, key_row, scale_one)
    qkv_part = scatter_rows(x, qkv_back)
    grad_one = team_sum(dot(qkv_back, w_qkv, NT), place)
    x_own, r_own = tokens.astype(F32), own(scale_one)
    tokens_grad = grad_after + grad_one - x_own * (r_own * r_own * jnp.mean(x_own * grad_one, axis=1, keepdims=True))

    def owned(a):
        pieces = [p.astype(F32) for p in team_exchange_late(a.astype(BF16), place)]
        high, low = place // 2, place % 2
        near = jnp.where(low == 0, jnp.stack(pieces[:2]), jnp.stack(pieces[1::-1]))
        away = jnp.where(low == 0, jnp.stack(pieces[2:]), jnp.stack(pieces[:1:-1]))
        return jnp.where(high == 0, jnp.concatenate([near, away], 0), jnp.concatenate([away, near], 0))

    def spread(a):
        return jnp.concatenate([a[k] for k in range(team)], axis=1)

    down_grad = spread(owned(down_part))
    feed_part = owned(feed_part)
    gate_sum, up_sum = spread(feed_part[:, :, :units]), spread(feed_part[:, :, units:])
    out_grad = spread(owned(out_part))
    qkv_part = owned(qkv_part)
    q_sum = spread(qkv_part[:, :, :kq])
    k_sum = spread(qkv_part[:, :, kq : 2 * kq])
    v_sum = spread(qkv_part[:, :, 2 * kq :])
    over = lambda w, g: jnp.sum(w.astype(F32) * g, axis=1)
    gain_feed_grad = over(gate_weight, gate_sum) + over(up_weight, up_sum)
    gain_mixer_grad = over(query_weight, q_sum) + over(key_weight, k_sum) + over(value_weight, v_sum)
    return (
        output,
        tokens_grad,
        gain_mixer_grad,
        q_sum * mixer_col,
        k_sum * mixer_col,
        v_sum * mixer_col,
        out_grad,
        gain_feed_grad,
        gate_sum * feed_col,
        up_sum * feed_col,
        down_grad,
    )


def solution(mesh):
    rows = P(("dp", "fsdp"), None)
    flat = P(("dp", "fsdp"))
    return jax.shard_map(
        body,
        mesh=mesh,
        in_specs=(rows, P("dp", None), flat, flat, rows, rows, rows, rows, flat, rows, rows, rows, rows),
        out_specs=(rows, rows, flat, rows, rows, rows, rows, flat, rows, rows, rows),
        check_vma=False,
    )
```

```python
import functools
import math

import jax
import jax.numpy as jnp
from jax import lax
from jax.experimental import pallas as pl
from jax.experimental.pallas import tpu as pltpu
from jax.sharding import PartitionSpec as P

FDIM = 16
VDIM = 64
EPS = 1e-05
TILE = 256
LANES = 128
SPARE = 8 * 1024 * 1024

F32 = jnp.float32
BF16 = jnp.bfloat16
NT = ((1,), (1,))
TN = ((0,), (0,))


def dot(a, b, dims=((1,), (0,))):
    return lax.dot_general(a, b, (dims, ((), ())), preferred_element_type=F32)


def shape(rows, cols, dtype):
    return jax.ShapeDtypeStruct((rows, cols), dtype)


def padded(dims, dtype):
    rows, cols = dims[-2:]
    return math.prod(dims[:-2]) * (rows + -rows % 16) * (cols + -cols % LANES) * jnp.dtype(dtype).itemsize


def call(kernel, outs, scalars, arrays, scratch=(), after=(), us=4, spare=SPARE):
    used = len(scalars) + len(arrays)

    def run(*refs):
        kernel(*refs[:used], *refs[used + len(after) :])

    smem = pl.BlockSpec(memory_space=pltpu.SMEM)
    vmem = pl.BlockSpec(memory_space=pltpu.VMEM)
    anywhere = pl.BlockSpec(memory_space=pl.ANY)
    held = sum(padded(a.shape, a.dtype) for a in (*arrays, *jax.tree.leaves(outs), *scratch))
    return pl.pallas_call(
        run,
        out_shape=outs,
        in_specs=[smem] * len(scalars) + [vmem] * len(arrays) + [anywhere] * len(after),
        out_specs=jax.tree.map(lambda _: vmem, outs),
        scratch_shapes=list(scratch),
        compiler_params=pltpu.CompilerParams(vmem_limit_bytes=held + spare),
        cost_estimate=pl.CostEstimate(flops=1, bytes_accessed=us * 3_000_000, transcendentals=0),
    )(*scalars, *arrays, *after)


def swap(a, axis, bit):
    n = lax.axis_size(axis)
    return lax.ppermute(a, axis, [(i, i ^ bit) for i in range(n)])


def part(a, start, size):
    return lax.dynamic_slice_in_dim(a, start, size, 0)


def pick(flag, one, two):
    return jnp.where(flag == 0, jnp.concatenate([one, two], 0), jnp.concatenate([two, one], 0))


def team_pieces(a):
    far = swap(a, "fsdp", 2)
    return a, swap(a, "fsdp", 1), far, swap(far, "fsdp", 1)


def blocks_of(a, place):
    rows = a.shape[0] // 4
    return [part(a, (place ^ k) * rows, rows) for k in range(4)]


def exchange(blocks):
    return [blocks[0]] + [swap(blocks[k], "fsdp", k) for k in (1, 2, 3)]


def in_order(pieces, place):
    high, low = place // 2, place % 2
    return pick(high, pick(low, pieces[0], pieces[1]), pick(low, pieces[2], pieces[3]))


def layout():
    block = jnp.arange(8, dtype=jnp.int32)
    if lax.axis_size("dp") != 8:
        return block, block
    at = lax.axis_index("dp")
    z, y = at // 2, at % 2
    return ((block % 2) ^ y) * 4 + ((block // 2) ^ z), 2 * ((block % 4) ^ z) + ((block // 4) ^ y)


def gather(a, axis):
    if lax.axis_size("dp") != 8:
        whole = lax.all_gather(a, "dp", axis=axis, tiled=True)
        half = whole.shape[axis] // 2
        return lax.slice_in_dim(whole, 0, half, axis=axis), lax.slice_in_dim(whole, half, 2 * half, axis=axis)
    mine = jnp.concatenate([a] + [swap(a, "dp", 2 * k) for k in (1, 2, 3)], axis)
    return mine, swap(mine, "dp", 1)


def lane_of(dims):
    return lax.broadcasted_iota(jnp.int32, dims, len(dims) - 1)


def query_cols(both):
    high = both.astype(BF16).astype(F32)
    low = both - high
    left = lane_of(both.shape) < 64
    one = jnp.where(left, high, pltpu.roll(low, 64, 1))
    two = jnp.where(left, high, 0.0)
    return jnp.concatenate([one.astype(BF16), two.astype(BF16)], axis=1)


def key_cols(both):
    high = both.astype(BF16).astype(F32)
    low = both - high
    left = lane_of(both.shape) < 64
    one = jnp.where(left, pltpu.roll(high, 64, 1), high)
    two = jnp.where(left, pltpu.roll(low, 64, 1), 0.0)
    return jnp.concatenate([one.astype(BF16), two.astype(BF16)], axis=1)


def head_only(a, h, width):
    lane = lane_of(a.shape)
    if width == FDIM:
        lane = lane % 64
    return jnp.where(lane // width == h, a, jnp.zeros_like(a))


def doc_starts(offsets_ref, i):
    place = i * TILE + lax.broadcasted_iota(jnp.int32, (TILE, 1), 0)
    start = jnp.zeros((TILE, 1), jnp.int32)
    for d in range(offsets_ref.shape[1]):
        first = offsets_ref[0, d]
        start = jnp.where(first <= place, jnp.maximum(start, first), start)
    return start


def allowed(start, row, i, j):
    ok = row >= start
    if i == j:
        place = i * TILE + lax.broadcasted_iota(jnp.int32, (TILE, TILE), 0)
        ok = ok & (row <= place)
    return ok


def forward_kernel(info, offsets_ref, t0, t1, t2, t3, wa, wb, xp, raw_ref, mixed_ref, exact_ref, den_ref, scale_ref, row_ref, qc, kc, vc):
    place = info[0]
    blocks = xp.shape[0] // TILE
    half = wa.shape[0]
    team_heads = vc.shape[1] // VDIM
    for k, t in enumerate((t0, t1, t2, t3)):
        block = place ^ k
        at = pl.ds(pl.multiple_of(block * TILE, TILE), TILE)
        x = t[:TILE, :]
        for p in range(8):
            xp[at, pl.ds(pl.multiple_of(info[8 + p] * LANES, LANES), LANES)] = x[:, p * LANES : (p + 1) * LANES]
        live = t[TILE : TILE + 16, :TILE].astype(F32)[:1, :]
        place_row = block * TILE + lane_of((1, TILE))
        row_ref[block] = jnp.broadcast_to(jnp.where(live > 0.5, place_row, -1), (8, TILE))
    for i in range(blocks):
        at = pl.ds(i * TILE, TILE)
        x = xp[at, :]
        wide = x.astype(F32)
        scale = lax.rsqrt(jnp.mean(wide * wide, axis=1, keepdims=True) + EPS)
        scale_ref[at, :] = jnp.broadcast_to(scale, (TILE, LANES))
        raw = (dot(x[:, :half], wa[:, : raw_ref.shape[1]]) + dot(x[:, half:], wb[:, : raw_ref.shape[1]])) * scale
        raw_ref[at, :] = raw
        both = raw[:, :LANES]
        qc[at, :] = query_cols(both)
        kc[at, :] = key_cols(both)
        vc[at, :] = raw[:, LANES:].astype(BF16)
    for i in range(blocks):
        at = pl.ds(i * TILE, TILE)
        start = doc_starts(offsets_ref, i)
        q = qc[at, :]
        result = jnp.zeros((TILE, vc.shape[1]), F32)
        dens = jnp.zeros((TILE, LANES), F32)
        for h in range(team_heads):
            total = jnp.zeros((TILE, vc.shape[1]), F32)
            den = jnp.zeros((TILE, 1), F32)
            for j in range(i + 1):
                there = pl.ds(j * TILE, TILE)
                s = dot(q, head_only(kc[there, :], h, FDIM), NT)
                kept = 1.0 + s * (0.25 + s * 0.03125)
                kept = jnp.where(allowed(start, row_ref[j][:1, :], i, j), kept, 0.0)
                den = den + jnp.sum(kept, axis=1, keepdims=True)
                total = total + dot(kept.astype(BF16), vc[there, :])
            result = jnp.where(lane_of(result.shape) // VDIM == h, total / den, result)
            dens = jnp.where(lane_of(dens.shape) == h, den, dens)
        exact_ref[at, :] = result
        mixed_ref[at, :] = result.astype(BF16)
        den_ref[at, :] = dens


def attend(info, offsets, tokens, wa, wb, width, after=()):
    length = 4 * TILE
    value = width - LANES
    model = tokens[0].shape[1]
    return call(
        forward_kernel,
        (
            shape(length, model, BF16),
            shape(length, width, F32),
            shape(length, value, BF16),
            shape(length, value, F32),
            shape(length, LANES, F32),
            shape(length, LANES, F32),
            jax.ShapeDtypeStruct((4, 8, TILE), jnp.int32),
        ),
        (info, offsets),
        (*tokens, wa, wb),
        [pltpu.VMEM((length, 256), BF16), pltpu.VMEM((length, 256), BF16), pltpu.VMEM((length, value), BF16)], after=after, us=9)


def backward_kernel(info, offsets_ref, raw_ref, g0, g1, g2, g3, wo, exact_ref, den_ref, row_ref, scale_ref, back_ref, gm, qc, kc, qr, kr, vc, acc):
    place = info[0]
    blocks = raw_ref.shape[0] // TILE
    team_heads = vc.shape[1] // VDIM
    mine_rows = pl.ds(pl.multiple_of(place * TILE, TILE), TILE)
    for k, g in enumerate((g0, g1, g2, g3)):
        at = pl.ds(pl.multiple_of((place ^ k) * TILE, TILE), TILE)
        gm[at, :] = dot(g[...], wo[mine_rows, :], NT)
    for i in range(blocks):
        at = pl.ds(i * TILE, TILE)
        raw = raw_ref[at, :]
        both = raw[:, :LANES]
        qc[at, :] = query_cols(both)
        kc[at, :] = key_cols(both)
        turned = pltpu.roll(both, 64, 1)
        left = lane_of(both.shape) < 64
        kr[at, :] = jnp.where(left, turned, 0.0).astype(BF16)
        qr[at, :] = jnp.where(left, 0.0, turned).astype(BF16)
        vc[at, :] = raw[:, LANES:].astype(BF16)
    acc[...] = jnp.zeros_like(acc)
    for i in range(blocks):
        at = pl.ds(i * TILE, TILE)
        start = doc_starts(offsets_ref, i)
        q = qc[at, :]
        grad = gm[at, :]
        product = grad * exact_ref[at, :]
        dens = den_ref[at, :]
        for h in range(team_heads):
            inverse = 1.0 / jnp.sum(jnp.where(lane_of(dens.shape) == h, dens, 0.0), axis=1, keepdims=True)
            numer = head_only(grad * inverse, h, VDIM).astype(BF16)
            denom = -jnp.sum(head_only(product, h, VDIM), axis=1, keepdims=True) * inverse
            mine = head_only(qr[at, :], h, FDIM)
            back = jnp.zeros((TILE, LANES), F32)
            for j in range(i + 1):
                there = pl.ds(j * TILE, TILE)
                s = dot(q, head_only(kc[there, :], h, FDIM), NT)
                ok = allowed(start, row_ref[j][:1, :], i, j)
                kept = jnp.where(ok, 1.0 + s * (0.25 + s * 0.03125), 0.0)
                inner = dot(numer, vc[there, :], NT) + denom
                inner = jnp.where(ok, inner * (0.25 + s * 0.0625), 0.0).astype(BF16)
                back = back + dot(inner, head_only(kr[there, :], h, FDIM))
                acc[there, :LANES] += dot(inner, mine, TN)
                acc[there, LANES:] += dot(kept.astype(BF16), numer, TN)
            acc[at, :LANES] += back
    for i in range(blocks):
        at = pl.ds(i * TILE, TILE)
        back_ref[at, :] = (acc[at, :] * scale_ref[at, :1]).astype(BF16)


def attend_back(info, offsets, raw, grads, wo, exact, den, row, scale, after=()):
    length, width = raw.shape
    value = width - LANES
    return call(
        backward_kernel,
        shape(length, width, BF16),
        (info, offsets),
        (raw, *grads, wo, exact, den, row, scale),
        [
            pltpu.VMEM((length, value), F32),
            pltpu.VMEM((length, 256), BF16),
            pltpu.VMEM((length, 256), BF16),
            pltpu.VMEM((length, LANES), BF16),
            pltpu.VMEM((length, LANES), BF16),
            pltpu.VMEM((length, value), BF16),
            pltpu.VMEM((length, width), F32),
        ],
        after=after, us=18)


def straight_kernel(cols, info, a, b, out):
    for n in range(8):
        source, first = (a, n * LANES) if n < 4 else (b, (n - 4) * LANES)
        out[pl.ds(pl.multiple_of(info[16 + n] * LANES, LANES), LANES), :] = source[first : first + LANES, cols:]


def whole_kernel(info, o0, o1, o2, o3, out):
    for k, o in enumerate((o0, o1, o2, o3)):
        out[:, pl.ds(pl.multiple_of((info[0] ^ k) * TILE, TILE), TILE)] = o[...]


def mix_kernel(info, t0, t1, t2, t3, m0, m1, m2, m3, wo, hidden_ref, own_ref, scale_ref, mixed):
    place = info[0]
    for k, m in enumerate((m0, m1, m2, m3)):
        mixed[:, pl.ds(pl.multiple_of((place ^ k) * TILE, TILE), TILE)] = m[...]
    for k, t in enumerate((t0, t1, t2, t3)):
        rows = pl.ds(pl.multiple_of((place ^ k) * TILE, TILE), TILE)
        total = t[:TILE, :].astype(F32) + dot(mixed[rows, :], wo[...])
        scale = lax.rsqrt(jnp.mean(total * total, axis=1, keepdims=True) + EPS)
        hidden_ref[k * TILE : (k + 1) * TILE, :] = (total * scale).astype(BF16)
        if k == 0:
            own_ref[...] = total
            scale_ref[...] = jnp.broadcast_to(scale, scale_ref.shape)


def feed_kernel(hidden_ref, c0, c1, c2, c3, w_ref, act_ref, turned_ref, give, far, keep, w):
    units = w.shape[0] // 3
    for p in range(w_ref.shape[0]):
        width = w_ref.shape[2]
        w[:, p * width : (p + 1) * width] = w_ref[p]
    gw, uw, dw = (w[n * units : (n + 1) * units, :] for n in range(3))
    outs = ((keep, 0), (give, 0), (far, 0), (give, TILE))
    for k, c in enumerate((c0, c1, c2, c3)):
        at = slice(k * TILE, (k + 1) * TILE)
        h = hidden_ref[at, :]
        gate = dot(h, gw, NT)
        lift = dot(h, uw, NT)
        grad = dot(c[...], dw, NT)
        sig = 1.0 / (1.0 + jnp.exp(-gate))
        silu = gate * sig
        act = (silu * lift).astype(BF16)
        gate_back = (grad * lift * (sig + silu * (1.0 - sig))).astype(BF16)
        lift_back = (grad * silu).astype(BF16)
        act_ref[at, :] = act
        out, first = outs[k]
        out[first : first + TILE, :] = (dot(gate_back, gw) + dot(lift_back, uw)).astype(out.dtype)
        turned_ref[:units, at] = gate_back.T
        turned_ref[units : 2 * units, at] = lift_back.T
        turned_ref[2 * units :, at] = act.T


def feed(hidden, cots, weights):
    rows, model = hidden.shape
    units = weights.shape[1] // 3
    return call(
        feed_kernel,
        (
            shape(rows, units, BF16),
            shape(3 * units, rows, BF16),
            shape(rows // 2, model, BF16),
            shape(rows // 4, model, F32),
            shape(rows // 4, model, F32),
        ),
        (),
        (hidden, *cots, weights),
        [pltpu.VMEM((3 * units, model), BF16)], us=15)


def feed_grad_kernel(numbers, info, hidden, *refs):
    cots, (turned, give, keep, whole) = refs[:-4], refs[-4:]
    units = turned.shape[0] // 3
    for at, number in enumerate(numbers):
        rows = slice(number * units, (number + 1) * units)
        if number < 2:
            total = dot(turned[rows, :], hidden[...])
        else:
            total = sum(dot(turned[rows, k * TILE : (k + 1) * TILE], c[...]) for k, c in enumerate(cots))
        width = total.shape[1] // 8
        half = total.shape[1] // 2
        for p in range(8):
            spot = pl.ds(pl.multiple_of(info[8 + p] * width, width), width)
            whole[:, spot] = total[:, p * width : (p + 1) * width]
        out = slice(at * units, (at + 1) * units)
        keep[out, :] = whole[:, :half].astype(BF16)
        give[out, :] = whole[:, half:].astype(BF16)


def feed_grad(info, numbers, hidden, cots, turned, after=()):
    units, model = turned.shape[0] // 3, hidden.shape[1]
    return call(
        functools.partial(feed_grad_kernel, numbers),
        (shape(len(numbers) * units, model // 2, BF16),) * 2,
        (info,),
        (hidden, *cots, turned),
        [pltpu.VMEM((units, model), F32)],
        after=after,
    )


def middle_kernel(keep, got, own, *sends):
    size = own.shape[1]
    own[...] = keep[:, :size].astype(F32) + got[:, :size].astype(F32)
    for k in (1, 2, 3):
        cols = slice(k * size, (k + 1) * size)
        sends[k - 1][...] = (keep[:, cols].astype(F32) + got[:, cols].astype(F32)).astype(BF16)


def middle(give, keep, after=()):
    units, half = keep.shape
    if lax.axis_size("dp") != 8:
        whole = jnp.concatenate([keep, give], axis=1).astype(F32)
        return [lax.psum_scatter(whole, "dp", scatter_dimension=1, tiled=True)]
    outs = (shape(units, half // 4, F32),) + (shape(units, half // 4, BF16),) * 3
    own, *sends = call(middle_kernel, outs, (), (keep, swap(give, "dp", 1)), after=after)
    return [own] + [swap(sends[k - 1], "dp", 2 * k) for k in (1, 2, 3)]


def sum_kernel(*refs):
    total = refs[0][...]
    for t in refs[1:-1]:
        total = total + t[...].astype(F32)
    refs[-1][...] = total


def sum_terms(terms, after=()):
    if len(terms) == 1:
        return terms[0]
    return call(sum_kernel, shape(*terms[0].shape, F32), (), tuple(terms), after=after)


def after_kernel(keep, first, got, after_ref, scale_ref, cot, grad_ref, low_ref):
    total = keep[...] + first[:TILE, :].astype(F32) + got[...].astype(F32)
    after = after_ref[...]
    scale = scale_ref[:, :1]
    inner = jnp.mean(after * total, axis=1, keepdims=True)
    grad = cot[...].astype(F32) + scale * total - after * (scale * scale * scale * inner)
    grad_ref[...] = grad
    low_ref[...] = grad.astype(BF16)


def tokens_kernel(info, keep, first, got, scale_ref, tokens, grad, out, straight):
    for p in range(8):
        spot = pl.ds(pl.multiple_of(info[8 + p] * LANES, LANES), LANES)
        straight[:, p * LANES : (p + 1) * LANES] = keep[:, spot] + first[:TILE, spot].astype(F32) + got[:, spot].astype(F32)
    total = straight[...]
    x = tokens[:TILE, :].astype(F32)
    scale = scale_ref[pl.ds(pl.multiple_of(info[0] * TILE, TILE), TILE), :][:, :1]
    out[...] = grad[...] + total - x * (scale * scale * jnp.mean(x * total, axis=1, keepdims=True))


def result_kernel(act, w_ref, give, far, keep):
    units = act.shape[1]
    width = w_ref.shape[2]
    for k, (out, first) in enumerate(((keep, 0), (give, 0), (far, 0), (give, TILE))):
        a = act[k * TILE : (k + 1) * TILE, :]
        for p in range(0, w_ref.shape[0], 2):
            w = jnp.concatenate([w_ref[p, 2 * units :, :], w_ref[p + 1, 2 * units :, :]], axis=1)
            out[first : first + TILE, p * width : (p + 2) * width] = dot(a, w).astype(out.dtype)


def pack_kernel(info, wq, wk, wv, wo, wg, wu, wd, mixer, feed, *outs):
    place = info[0]
    scaled = lambda w, gain: (w[...].astype(F32) * gain[...]).astype(BF16)
    arrays = [scaled(w, mixer) for w in (wq, wk, wv)] + [wo[...]] + [scaled(w, feed) for w in (wg, wu)] + [wd[...]]
    for k, out in enumerate(outs):
        member = place ^ k
        first = 0
        for a in arrays:
            width = a.shape[1] // 4
            best = a[:, :width]
            for q in (1, 2, 3):
                best = jnp.where(member == q, a[:, q * width : (q + 1) * width], best)
            out[:, first : first + width] = best
            first += width


def cut_kernel(first, turn, info, p0, p1, p2, p3, out, whole):
    rows, width = p0.shape[0], whole.shape[1]
    for k, p in enumerate((p0, p1, p2, p3)):
        at = pl.ds(pl.multiple_of((info[0] ^ k) * rows, rows), rows)
        whole[at, :] = p[:, first : first + width].astype(F32)
    a = whole[...]
    out[...] = (a.T if turn else a).astype(BF16)


def cut(info, pieces, first, width, turn, after=(), us=2):
    rows = 4 * pieces[0].shape[0]
    if lax.axis_size("dp") != 8:
        a = in_order(pieces, info[0])[:, first : first + width]
        return a.T if turn else a
    out = shape(width, rows, BF16) if turn else shape(rows, width, BF16)
    return call(
        functools.partial(cut_kernel, first, turn), out, (info,), tuple(pieces), [pltpu.VMEM((rows, width), F32)], after=after, us=us
    )


def pack_tokens_kernel(tokens, live, out):
    height = tokens.shape[0]
    out[:height, :] = tokens[...]
    out[height:, :] = jnp.broadcast_to(live[...], out[height:, :].shape).astype(BF16)


def copy_kernel(a, out):
    out[...] = a[...]


def finish_kernel(info, own, t1, t2, t3, e0, e1, e2, e3, whole):
    rows = e0.shape[0] // 3
    units = own.shape[0] // 3
    for n in range(3):
        at = slice(n * units, (n + 1) * units)
        total = own[at, :]
        for t in (t1, t2, t3):
            total = total + t[at, :].astype(F32)
        whole[...] = total.T
        for k, out in enumerate((e0, e1, e2, e3)):
            there = pl.ds(pl.multiple_of((info[0] ^ k) * rows, rows), rows)
            out[n * rows : (n + 1) * rows, :] = whole[there, :].astype(BF16)


def finish(info, place, terms, after=()):
    units, rows = terms[0].shape[0] // 3, terms[0].shape[1]
    if len(terms) == 1:
        blocks = [blocks_of(terms[0][n * units : (n + 1) * units].T.astype(BF16), place) for n in range(3)]
        return [jnp.concatenate([b[k] for b in blocks], axis=0) for k in range(4)]
    return call(
        finish_kernel,
        (shape(3 * rows // 4, units, BF16),) * 4,
        (info,),
        tuple(terms),
        [pltpu.VMEM((rows, units), F32)],
        after=after,
    )


def far_kernel(far, got, out):
    out[...] = (far[...] + got[out.shape[0] :, :].astype(F32)).astype(BF16)


def output_kernel(after, keep, first, got, out):
    out[...] = after[...] + keep[...] + first[: out.shape[0], :].astype(F32) + got[...].astype(F32)


def inputs_kernel(info, back, wa, wb, give, far, keep):
    half = wa.shape[0]
    for k, (out, first) in enumerate(((keep, 0), (give, 0), (far, 0), (give, TILE))):
        a = back[pl.ds(pl.multiple_of((info[0] ^ k) * TILE, TILE), TILE), :]
        out[first : first + TILE, :half] = dot(a, wa[:, : a.shape[1]], NT).astype(out.dtype)
        out[first : first + TILE, half:] = dot(a, wb[:, : a.shape[1]], NT).astype(out.dtype)


def output_weight_kernel(info, m0, m1, m2, m3, g0, g1, g2, g3, out):
    place = info[0]
    mine = pl.ds(pl.multiple_of(place * TILE, TILE), TILE)
    for k, m in enumerate((m0, m1, m2, m3)):
        total = jnp.zeros((m.shape[1], TILE), F32)
        for b, g in enumerate((g0, g1, g2, g3)):
            rows = pl.ds(pl.multiple_of((place ^ b) * TILE, TILE), TILE)
            total = total + dot(m[rows, :], g[:, mine], TN)
        for side in (0, 1):
            spot = info[8 + 2 * (place ^ k) + side]
            out[pl.ds(pl.multiple_of(spot * LANES, LANES), LANES), :] = total[side * LANES : (side + 1) * LANES].astype(BF16)


def late_give_kernel(x, back, other, out):
    half, width = out.shape[0], back.shape[1]
    out[:, :width] = dot(x[:, half:], back[...], TN).astype(BF16)
    out[:, width:] = other[half:, :]


def late_middle_kernel(x, back, other, got, own, s1, s2, s3):
    half, width = got.shape[0], back.shape[1]
    rows = half // 4
    one = dot(x[:, :half], back[...], TN) + got[:, :width].astype(F32)
    two = other[:half, :].astype(F32) + got[:, width:].astype(F32)
    own[:, :width] = one[:rows]
    own[:, width:] = two[:rows]
    for k, out in ((1, s1), (2, s2), (3, s3)):
        out[:, :width] = one[k * rows : (k + 1) * rows].astype(BF16)
        out[:, width:] = two[k * rows : (k + 1) * rows].astype(BF16)


def late_give(x, back, other):
    half, cols = x.shape[1] // 2, back.shape[1] + other.shape[1]
    return call(late_give_kernel, shape(half, cols, BF16), (), (x, back, other))


def late_middle(x, back, other, give, after):
    half, cols = x.shape[1] // 2, back.shape[1] + other.shape[1]
    if lax.axis_size("dp") != 8:
        keep = jnp.concatenate([dot(x[:, :half], back, TN), other[:half].astype(F32)], axis=1)
        whole = jnp.concatenate([keep, give.astype(F32)], axis=0)
        return [lax.psum_scatter(whole, "dp", scatter_dimension=0, tiled=True)]
    own, *sends = call(
        late_middle_kernel,
        (shape(half // 4, cols, F32),) + (shape(half // 4, cols, BF16),) * 3,
        (),
        (x, back, other, swap(give, "dp", 1)),
        after=after,
    )
    return [own] + [swap(sends[k - 1], "dp", 2 * k) for k in (1, 2, 3)]


def body(
    tokens,
    offsets,
    live_tokens,
    gain_mixer,
    query_weight,
    key_weight,
    value_weight,
    output_weight,
    gain_feed,
    gate_weight,
    up_weight,
    down_weight,
    cotangent,
):
    team = lax.axis_size("fsdp")
    place = lax.axis_index("fsdp")
    height, model = tokens.shape
    length = height * team
    units = gate_weight.shape[1] // team
    kq, kv, ko = (w.shape[1] // team for w in (query_weight, value_weight, output_weight))
    width = 2 * kq + kv
    own_rows = gain_mixer.shape[0]
    slots, blocks = layout()
    info = jnp.concatenate([jnp.full((8,), place, jnp.int32), slots, blocks])

    mixer_col = gain_mixer.astype(F32)[:, None]
    feed_col = gain_feed.astype(F32)[:, None]
    packs = call(
        pack_kernel,
        (shape(own_rows, width + ko + 3 * units, BF16),) * 4,
        (info,),
        (query_weight, key_weight, value_weight, output_weight, gate_weight, up_weight, down_weight, mixer_col, feed_col),
        spare=7 * SPARE,
    )
    packs = exchange(packs)
    first = cut(info, packs, 0, width + ko, False, us=2)
    wa, wb = gather(first, 0)
    feed_w = lax.all_gather(cut(info, packs, width + ko, 3 * units, True, after=(first,), us=2), "dp", axis=0)
    live_row = jnp.pad(live_tokens.astype(F32)[None, :], ((0, 0), (0, model - height)))
    packed = team_pieces(
        call(pack_tokens_kernel, shape(height + 16, model, BF16), (), (tokens, live_row), after=tuple(packs[1:]), us=2)
    )
    straight = call(functools.partial(straight_kernel, width), shape(model, ko, BF16), (info,), (wa, wb), us=2)
    xp, raw, mixed, exact, den, scale_one, row = attend(info, offsets, packed, wa, wb, width, after=(straight,))
    outs = team_pieces(straight)
    wo = call(whole_kernel, shape(model, model, BF16), (info,), tuple(outs), us=3)

    mixes = team_pieces(mixed)
    cots = team_pieces(call(copy_kernel, shape(height, model, BF16), (), (cotangent,), after=(packed[2],)))
    hidden, after, scale_two = call(
        mix_kernel,
        (shape(length, model, BF16), shape(height, model, F32), shape(height, LANES, F32)),
        (info,),
        (*packed, *mixes, wo),
        [pltpu.VMEM((length, model), BF16)], us=7)

    act, turned, give, far, keep = feed(hidden, cots, feed_w)
    got = swap(give, "fsdp", 1)
    far = call(far_kernel, shape(height, model, BF16), (), (far, got))
    give_f, keep_f = feed_grad(info, (0, 1, 2), hidden, cots, turned, after=(far,))
    grad_after, low = call(
        after_kernel,
        (shape(height, model, F32), shape(height, model, BF16)),
        (),
        (keep, got, swap(far, "fsdp", 2), after, scale_two, cotangent),
        after=(give_f,),
    )
    grads = team_pieces(low)

    qkv_back = attend_back(info, offsets, raw, grads, wo, exact, den, row, scale_one)
    out_part = call(output_weight_kernel, shape(model, ko, BF16), (info,), (*mixes, *grads), after=(qkv_back,))
    give_l = late_give(xp, qkv_back, out_part)
    give1, far1, keep1 = call(
        inputs_kernel,
        (shape(2 * height, model, BF16), shape(height, model, F32), shape(height, model, F32)),
        (info,),
        (qkv_back, wa, wb),
        after=(give_l,),
    )
    got1 = swap(give1, "fsdp", 1)
    give2, far2, keep2 = call(
        result_kernel,
        (shape(2 * height, model, BF16), shape(height, model, F32), shape(height, model, F32)),
        (),
        (act, feed_w),
        after=(give1,),
    )
    got2 = swap(give2, "fsdp", 1)
    far1 = call(far_kernel, shape(height, model, BF16), (), (far1, got1), after=(give2,))
    far2 = call(far_kernel, shape(height, model, BF16), (), (far2, got2), after=(far1,))
    terms_f = middle(give_f, keep_f, after=(far2,))
    terms_l = late_middle(xp, qkv_back, out_part, give_l, after=(terms_f[0],))
    tokens_grad = call(
        tokens_kernel,
        shape(height, model, F32),
        (info,),
        (keep1, got1, swap(far1, "fsdp", 2), scale_one, packed[0], grad_after),
        [pltpu.VMEM((height, model), F32)],
        after=(terms_l[0],),
    )
    output = call(
        output_kernel,
        shape(height, model, F32),
        (),
        (after, keep2, got2, swap(far2, "fsdp", 2)),
        after=(tokens_grad,),
    )
    feed_pieces = finish(info, place, terms_f, (output,))
    late = sum_terms(terms_l, after=(feed_pieces[0],))

    def spread(pieces):
        near = jnp.where(place % 2 == 0, jnp.stack(pieces[:2]), jnp.stack(pieces[1::-1]))
        away = jnp.where(place % 2 == 0, jnp.stack(pieces[2:]), jnp.stack(pieces[:1:-1]))
        whole = jnp.where(place // 2 == 0, jnp.concatenate([near, away], 0), jnp.concatenate([away, near], 0))
        return lambda r, a, b: jnp.concatenate([whole[k, r : r + own_rows, a:b] for k in range(team)], axis=1).astype(F32)

    late = spread(exchange(blocks_of(late.astype(BF16), place)))
    q_sum, k_sum, v_sum = late(0, 0, kq), late(0, kq, 2 * kq), late(0, 2 * kq, width)
    out_grad = late(0, width, width + ko)
    wide = spread(exchange(feed_pieces))
    gate_sum, up_sum, down_grad = wide(0, 0, units), wide(own_rows, 0, units), wide(2 * own_rows, 0, units)
    over = lambda w, g: jnp.sum(w.astype(F32) * g, axis=1)
    gain_feed_grad = over(gate_weight, gate_sum) + over(up_weight, up_sum)
    gain_mixer_grad = over(query_weight, q_sum) + over(key_weight, k_sum) + over(value_weight, v_sum)
    return (
        output,
        tokens_grad,
        gain_mixer_grad,
        q_sum * mixer_col,
        k_sum * mixer_col,
        v_sum * mixer_col,
        out_grad,
        gain_feed_grad,
        gate_sum * feed_col,
        up_sum * feed_col,
        down_grad,
    )


def solution(mesh):
    rows = P(("dp", "fsdp"), None)
    flat = P(("dp", "fsdp"))
    return jax.shard_map(
        body,
        mesh=mesh,
        in_specs=(rows, P("dp", None), flat, flat, rows, rows, rows, rows, flat, rows, rows, rows, rows),
        out_specs=(rows, rows, flat, rows, rows, rows, rows, flat, rows, rows, rows),
        check_vma=False,
    )
```

```python
import functools
import math

import jax
import jax.numpy as jnp
from jax import lax
from jax.experimental import pallas as pl
from jax.experimental.pallas import tpu as pltpu
from jax.sharding import PartitionSpec as P

FDIM = 16
VDIM = 64
EPS = 1e-05
TILE = 256
LANES = 128
SPARE = 8 * 1024 * 1024

F32 = jnp.float32
BF16 = jnp.bfloat16
NT = ((1,), (1,))
TN = ((0,), (0,))


def dot(a, b, dims=((1,), (0,))):
    return lax.dot_general(a, b, (dims, ((), ())), preferred_element_type=F32)


def shape(rows, cols, dtype):
    return jax.ShapeDtypeStruct((rows, cols), dtype)


def padded(dims, dtype):
    rows, cols = dims[-2:]
    return math.prod(dims[:-2]) * (rows + -rows % 16) * (cols + -cols % LANES) * jnp.dtype(dtype).itemsize


def call(kernel, outs, scalars, arrays, scratch=(), after=(), us=4, spare=SPARE):
    used = len(scalars) + len(arrays)

    def run(*refs):
        kernel(*refs[:used], *refs[used + len(after) :])

    smem = pl.BlockSpec(memory_space=pltpu.SMEM)
    vmem = pl.BlockSpec(memory_space=pltpu.VMEM)
    anywhere = pl.BlockSpec(memory_space=pl.ANY)
    held = sum(padded(a.shape, a.dtype) for a in (*arrays, *jax.tree.leaves(outs), *scratch))
    return pl.pallas_call(
        run,
        out_shape=outs,
        in_specs=[smem] * len(scalars) + [vmem] * len(arrays) + [anywhere] * len(after),
        out_specs=jax.tree.map(lambda _: vmem, outs),
        scratch_shapes=list(scratch),
        compiler_params=pltpu.CompilerParams(vmem_limit_bytes=held + spare),
        cost_estimate=pl.CostEstimate(flops=1, bytes_accessed=us * 3_000_000, transcendentals=0),
    )(*scalars, *arrays, *after)


def swap(a, axis, bit):
    n = lax.axis_size(axis)
    return lax.ppermute(a, axis, [(i, i ^ bit) for i in range(n)])


def part(a, start, size):
    return lax.dynamic_slice_in_dim(a, start, size, 0)


def pick(flag, one, two):
    return jnp.where(flag == 0, jnp.concatenate([one, two], 0), jnp.concatenate([two, one], 0))


def team_pieces(a):
    far = swap(a, "fsdp", 2)
    return a, swap(a, "fsdp", 1), far, swap(far, "fsdp", 1)


def blocks_of(a, place):
    rows = a.shape[0] // 4
    return [part(a, (place ^ k) * rows, rows) for k in range(4)]


def exchange(blocks):
    return [blocks[0]] + [swap(blocks[k], "fsdp", k) for k in (1, 2, 3)]


def in_order(pieces, place):
    high, low = place // 2, place % 2
    return pick(high, pick(low, pieces[0], pieces[1]), pick(low, pieces[2], pieces[3]))


def layout():
    block = jnp.arange(8, dtype=jnp.int32)
    if lax.axis_size("dp") != 8:
        return block, block
    at = lax.axis_index("dp")
    z, y = at // 2, at % 2
    return ((block % 2) ^ y) * 4 + ((block // 2) ^ z), 2 * ((block % 4) ^ z) + ((block // 4) ^ y)


def gather(a, axis):
    if lax.axis_size("dp") != 8:
        whole = lax.all_gather(a, "dp", axis=axis, tiled=True)
        half = whole.shape[axis] // 2
        return lax.slice_in_dim(whole, 0, half, axis=axis), lax.slice_in_dim(whole, half, 2 * half, axis=axis)
    mine = jnp.concatenate([a] + [swap(a, "dp", 2 * k) for k in (1, 2, 3)], axis)
    return mine, swap(mine, "dp", 1)


def lane_of(dims):
    return lax.broadcasted_iota(jnp.int32, dims, len(dims) - 1)


def query_cols(both):
    high = both.astype(BF16).astype(F32)
    low = both - high
    left = lane_of(both.shape) < 64
    one = jnp.where(left, high, pltpu.roll(low, 64, 1))
    two = jnp.where(left, high, 0.0)
    return jnp.concatenate([one.astype(BF16), two.astype(BF16)], axis=1)


def key_cols(both):
    high = both.astype(BF16).astype(F32)
    low = both - high
    left = lane_of(both.shape) < 64
    one = jnp.where(left, pltpu.roll(high, 64, 1), high)
    two = jnp.where(left, pltpu.roll(low, 64, 1), 0.0)
    return jnp.concatenate([one.astype(BF16), two.astype(BF16)], axis=1)


def head_only(a, h, width):
    lane = lane_of(a.shape)
    if width == FDIM:
        lane = lane % 64
    return jnp.where(lane // width == h, a, jnp.zeros_like(a))


def doc_starts(offsets_ref, i):
    place = i * TILE + lax.broadcasted_iota(jnp.int32, (TILE, 1), 0)
    start = jnp.zeros((TILE, 1), jnp.int32)
    for d in range(offsets_ref.shape[1]):
        first = offsets_ref[0, d]
        start = jnp.where(first <= place, jnp.maximum(start, first), start)
    return start


def allowed(start, row, i, j):
    ok = row >= start
    if i == j:
        place = i * TILE + lax.broadcasted_iota(jnp.int32, (TILE, TILE), 0)
        ok = ok & (row <= place)
    return ok


def forward_kernel(info, offsets_ref, t0, t1, t2, t3, wa, wb, xp, raw_ref, mixed_ref, exact_ref, den_ref, scale_ref, row_ref, qc, kc, vc):
    place = info[0]
    blocks = xp.shape[0] // TILE
    half = wa.shape[0]
    team_heads = vc.shape[1] // VDIM
    for k, t in enumerate((t0, t1, t2, t3)):
        block = place ^ k
        at = pl.ds(pl.multiple_of(block * TILE, TILE), TILE)
        x = t[:TILE, :]
        for p in range(8):
            xp[at, pl.ds(pl.multiple_of(info[8 + p] * LANES, LANES), LANES)] = x[:, p * LANES : (p + 1) * LANES]
        live = t[TILE : TILE + 16, :TILE].astype(F32)[:1, :]
        place_row = block * TILE + lane_of((1, TILE))
        row_ref[block] = jnp.broadcast_to(jnp.where(live > 0.5, place_row, -1), (8, TILE))
    for i in range(blocks):
        at = pl.ds(i * TILE, TILE)
        x = xp[at, :]
        wide = x.astype(F32)
        scale = lax.rsqrt(jnp.mean(wide * wide, axis=1, keepdims=True) + EPS)
        scale_ref[at, :] = jnp.broadcast_to(scale, (TILE, LANES))
        raw = (dot(x[:, :half], wa[:, : raw_ref.shape[1]]) + dot(x[:, half:], wb[:, : raw_ref.shape[1]])) * scale
        raw_ref[at, :] = raw
        both = raw[:, :LANES]
        qc[at, :] = query_cols(both)
        kc[at, :] = key_cols(both)
        vc[at, :] = raw[:, LANES:].astype(BF16)
    for i in range(blocks):
        at = pl.ds(i * TILE, TILE)
        start = doc_starts(offsets_ref, i)
        q = qc[at, :]
        result = jnp.zeros((TILE, vc.shape[1]), F32)
        dens = jnp.zeros((TILE, LANES), F32)
        for h in range(team_heads):
            total = jnp.zeros((TILE, vc.shape[1]), F32)
            den = jnp.zeros((TILE, 1), F32)
            for j in range(i + 1):
                there = pl.ds(j * TILE, TILE)
                s = dot(q, head_only(kc[there, :], h, FDIM), NT)
                kept = 1.0 + s * (0.25 + s * 0.03125)
                kept = jnp.where(allowed(start, row_ref[j][:1, :], i, j), kept, 0.0)
                den = den + jnp.sum(kept, axis=1, keepdims=True)
                total = total + dot(kept.astype(BF16), vc[there, :])
            result = jnp.where(lane_of(result.shape) // VDIM == h, total / den, result)
            dens = jnp.where(lane_of(dens.shape) == h, den, dens)
        exact_ref[at, :] = result
        mixed_ref[at, :] = result.astype(BF16)
        den_ref[at, :] = dens


def attend(info, offsets, tokens, wa, wb, width, after=()):
    length = 4 * TILE
    value = width - LANES
    model = tokens[0].shape[1]
    return call(
        forward_kernel,
        (
            shape(length, model, BF16),
            shape(length, width, F32),
            shape(length, value, BF16),
            shape(length, value, F32),
            shape(length, LANES, F32),
            shape(length, LANES, F32),
            jax.ShapeDtypeStruct((4, 8, TILE), jnp.int32),
        ),
        (info, offsets),
        (*tokens, wa, wb),
        [pltpu.VMEM((length, 256), BF16), pltpu.VMEM((length, 256), BF16), pltpu.VMEM((length, value), BF16)], after=after, us=9)


def backward_kernel(info, offsets_ref, raw_ref, g0, g1, g2, g3, wo, exact_ref, den_ref, row_ref, scale_ref, xp, m0, m1, m2, m3, back_ref, give_ref, keep_ref, gm, other, qc, kc, qr, kr, vc, acc):
    place = info[0]
    blocks = raw_ref.shape[0] // TILE
    team_heads = vc.shape[1] // VDIM
    mine_rows = pl.ds(pl.multiple_of(place * TILE, TILE), TILE)
    for k, g in enumerate((g0, g1, g2, g3)):
        at = pl.ds(pl.multiple_of((place ^ k) * TILE, TILE), TILE)
        gm[at, :] = dot(g[...], wo[mine_rows, :], NT)
    for i in range(blocks):
        at = pl.ds(i * TILE, TILE)
        raw = raw_ref[at, :]
        both = raw[:, :LANES]
        qc[at, :] = query_cols(both)
        kc[at, :] = key_cols(both)
        turned = pltpu.roll(both, 64, 1)
        left = lane_of(both.shape) < 64
        kr[at, :] = jnp.where(left, turned, 0.0).astype(BF16)
        qr[at, :] = jnp.where(left, 0.0, turned).astype(BF16)
        vc[at, :] = raw[:, LANES:].astype(BF16)
    acc[...] = jnp.zeros_like(acc)
    for i in range(blocks):
        at = pl.ds(i * TILE, TILE)
        start = doc_starts(offsets_ref, i)
        q = qc[at, :]
        grad = gm[at, :]
        product = grad * exact_ref[at, :]
        dens = den_ref[at, :]
        for h in range(team_heads):
            inverse = 1.0 / jnp.sum(jnp.where(lane_of(dens.shape) == h, dens, 0.0), axis=1, keepdims=True)
            numer = head_only(grad * inverse, h, VDIM).astype(BF16)
            denom = -jnp.sum(head_only(product, h, VDIM), axis=1, keepdims=True) * inverse
            mine = head_only(qr[at, :], h, FDIM)
            back = jnp.zeros((TILE, LANES), F32)
            for j in range(i + 1):
                there = pl.ds(j * TILE, TILE)
                s = dot(q, head_only(kc[there, :], h, FDIM), NT)
                ok = allowed(start, row_ref[j][:1, :], i, j)
                kept = jnp.where(ok, 1.0 + s * (0.25 + s * 0.03125), 0.0)
                inner = dot(numer, vc[there, :], NT) + denom
                inner = jnp.where(ok, inner * (0.25 + s * 0.0625), 0.0).astype(BF16)
                back = back + dot(inner, head_only(kr[there, :], h, FDIM))
                acc[there, :LANES] += dot(inner, mine, TN)
                acc[there, LANES:] += dot(kept.astype(BF16), numer, TN)
            acc[at, :LANES] += back
    for i in range(blocks):
        at = pl.ds(i * TILE, TILE)
        back_ref[at, :] = (acc[at, :] * scale_ref[at, :1]).astype(BF16)
    mine = pl.ds(pl.multiple_of(place * TILE, TILE), TILE)
    for k, m in enumerate((m0, m1, m2, m3)):
        total = jnp.zeros((m.shape[1], TILE), F32)
        for b, g in enumerate((g0, g1, g2, g3)):
            rows = pl.ds(pl.multiple_of((place ^ b) * TILE, TILE), TILE)
            total = total + dot(m[rows, :], g[:, mine], TN)
        for side in (0, 1):
            spot = info[8 + 2 * (place ^ k) + side]
            other[pl.ds(pl.multiple_of(spot * LANES, LANES), LANES), :] = total[side * LANES : (side + 1) * LANES].astype(BF16)
    half, width = give_ref.shape[0], back_ref.shape[1]
    give_ref[:, :width] = dot(xp[:, half:], back_ref[...], TN).astype(BF16)
    give_ref[:, width:] = other[half:, :]
    keep_ref[...] = other[:half, :]


def attend_back(info, offsets, raw, grads, wo, exact, den, row, scale, xp, mixes, after=()):
    length, width = raw.shape
    model, cols = xp.shape[1], grads[0].shape[1] // 4
    value = width - LANES
    return call(
        backward_kernel,
        (
            shape(length, width, BF16),
            shape(model // 2, width + cols, BF16),
            shape(model // 2, cols, BF16),
        ),
        (info, offsets),
        (raw, *grads, wo, exact, den, row, scale, xp, *mixes),
        [
            pltpu.VMEM((length, value), F32),
            pltpu.VMEM((model, cols), BF16),
            pltpu.VMEM((length, 256), BF16),
            pltpu.VMEM((length, 256), BF16),
            pltpu.VMEM((length, LANES), BF16),
            pltpu.VMEM((length, LANES), BF16),
            pltpu.VMEM((length, value), BF16),
            pltpu.VMEM((length, width), F32),
        ],
        after=after, us=18)


def straight_kernel(cols, info, a, b, out):
    for n in range(8):
        source, first = (a, n * LANES) if n < 4 else (b, (n - 4) * LANES)
        out[pl.ds(pl.multiple_of(info[16 + n] * LANES, LANES), LANES), :] = source[first : first + LANES, cols:]


def whole_kernel(info, o0, o1, o2, o3, out):
    for k, o in enumerate((o0, o1, o2, o3)):
        out[:, pl.ds(pl.multiple_of((info[0] ^ k) * TILE, TILE), TILE)] = o[...]


def mix_kernel(info, t0, t1, t2, t3, m0, m1, m2, m3, wo, hidden_ref, own_ref, scale_ref, mixed):
    place = info[0]
    for k, m in enumerate((m0, m1, m2, m3)):
        mixed[:, pl.ds(pl.multiple_of((place ^ k) * TILE, TILE), TILE)] = m[...]
    for k, t in enumerate((t0, t1, t2, t3)):
        rows = pl.ds(pl.multiple_of((place ^ k) * TILE, TILE), TILE)
        total = t[:TILE, :].astype(F32) + dot(mixed[rows, :], wo[...])
        scale = lax.rsqrt(jnp.mean(total * total, axis=1, keepdims=True) + EPS)
        hidden_ref[k * TILE : (k + 1) * TILE, :] = (total * scale).astype(BF16)
        if k == 0:
            own_ref[...] = total
            scale_ref[...] = jnp.broadcast_to(scale, scale_ref.shape)


def feed_kernel(hidden_ref, c0, c1, c2, c3, w_ref, act_ref, turned_ref, give, far, keep, w):
    units = w.shape[0] // 3
    for p in range(w_ref.shape[0]):
        width = w_ref.shape[2]
        w[:, p * width : (p + 1) * width] = w_ref[p]
    gw, uw, dw = (w[n * units : (n + 1) * units, :] for n in range(3))
    outs = ((keep, 0), (give, 0), (far, 0), (give, TILE))
    for k, c in enumerate((c0, c1, c2, c3)):
        at = slice(k * TILE, (k + 1) * TILE)
        h = hidden_ref[at, :]
        gate = dot(h, gw, NT)
        lift = dot(h, uw, NT)
        grad = dot(c[...], dw, NT)
        sig = 1.0 / (1.0 + jnp.exp(-gate))
        silu = gate * sig
        act = (silu * lift).astype(BF16)
        gate_back = (grad * lift * (sig + silu * (1.0 - sig))).astype(BF16)
        lift_back = (grad * silu).astype(BF16)
        act_ref[at, :] = act
        out, first = outs[k]
        out[first : first + TILE, :] = (dot(gate_back, gw) + dot(lift_back, uw)).astype(out.dtype)
        turned_ref[:units, at] = gate_back.T
        turned_ref[units : 2 * units, at] = lift_back.T
        turned_ref[2 * units :, at] = act.T


def feed(hidden, cots, weights):
    rows, model = hidden.shape
    units = weights.shape[1] // 3
    return call(
        feed_kernel,
        (
            shape(rows, units, BF16),
            shape(3 * units, rows, BF16),
            shape(rows // 2, model, BF16),
            shape(rows // 4, model, F32),
            shape(rows // 4, model, F32),
        ),
        (),
        (hidden, *cots, weights),
        [pltpu.VMEM((3 * units, model), BF16)], us=15)


def feed_grad_kernel(numbers, info, hidden, *refs):
    cots, (turned, give, keep, whole) = refs[:-4], refs[-4:]
    units = turned.shape[0] // 3
    for at, number in enumerate(numbers):
        rows = slice(number * units, (number + 1) * units)
        if number < 2:
            total = dot(turned[rows, :], hidden[...])
        else:
            total = sum(dot(turned[rows, k * TILE : (k + 1) * TILE], c[...]) for k, c in enumerate(cots))
        width = total.shape[1] // 8
        half = total.shape[1] // 2
        for p in range(8):
            spot = pl.ds(pl.multiple_of(info[8 + p] * width, width), width)
            whole[:, spot] = total[:, p * width : (p + 1) * width]
        out = slice(at * units, (at + 1) * units)
        keep[out, :] = whole[:, :half].astype(BF16)
        give[out, :] = whole[:, half:].astype(BF16)


def feed_grad(info, numbers, hidden, cots, turned, after=()):
    units, model = turned.shape[0] // 3, hidden.shape[1]
    return call(
        functools.partial(feed_grad_kernel, numbers),
        (shape(len(numbers) * units, model // 2, BF16),) * 2,
        (info,),
        (hidden, *cots, turned),
        [pltpu.VMEM((units, model), F32)],
        after=after,
    )


def middle_kernel(keep, got, own, *sends):
    size = own.shape[1]
    own[...] = keep[:, :size].astype(F32) + got[:, :size].astype(F32)
    for k in (1, 2, 3):
        cols = slice(k * size, (k + 1) * size)
        sends[k - 1][...] = (keep[:, cols].astype(F32) + got[:, cols].astype(F32)).astype(BF16)


def middle(give, keep, after=()):
    units, half = keep.shape
    if lax.axis_size("dp") != 8:
        whole = jnp.concatenate([keep, give], axis=1).astype(F32)
        return [lax.psum_scatter(whole, "dp", scatter_dimension=1, tiled=True)]
    outs = (shape(units, half // 4, F32),) + (shape(units, half // 4, BF16),) * 3
    own, *sends = call(middle_kernel, outs, (), (keep, swap(give, "dp", 1)), after=after)
    return [own] + [swap(sends[k - 1], "dp", 2 * k) for k in (1, 2, 3)]


def sum_kernel(*refs):
    total = refs[0][...]
    for t in refs[1:-1]:
        total = total + t[...].astype(F32)
    refs[-1][...] = total


def sum_terms(terms, after=()):
    if len(terms) == 1:
        return terms[0]
    return call(sum_kernel, shape(*terms[0].shape, F32), (), tuple(terms), after=after)


def after_kernel(keep, first, got, after_ref, scale_ref, cot, grad_ref, low_ref):
    total = keep[...] + first[:TILE, :].astype(F32) + got[...].astype(F32)
    after = after_ref[...]
    scale = scale_ref[:, :1]
    inner = jnp.mean(after * total, axis=1, keepdims=True)
    grad = cot[...].astype(F32) + scale * total - after * (scale * scale * scale * inner)
    grad_ref[...] = grad
    low_ref[...] = grad.astype(BF16)


def tokens_kernel(info, keep, first, got, scale_ref, tokens, grad, out, straight):
    for p in range(8):
        spot = pl.ds(pl.multiple_of(info[8 + p] * LANES, LANES), LANES)
        straight[:, p * LANES : (p + 1) * LANES] = keep[:, spot] + first[:TILE, spot].astype(F32) + got[:, spot].astype(F32)
    total = straight[...]
    x = tokens[:TILE, :].astype(F32)
    scale = scale_ref[pl.ds(pl.multiple_of(info[0] * TILE, TILE), TILE), :][:, :1]
    out[...] = grad[...] + total - x * (scale * scale * jnp.mean(x * total, axis=1, keepdims=True))


def result_kernel(act, w_ref, give, far, keep):
    units = act.shape[1]
    width = w_ref.shape[2]
    for k, (out, first) in enumerate(((keep, 0), (give, 0), (far, 0), (give, TILE))):
        a = act[k * TILE : (k + 1) * TILE, :]
        for p in range(0, w_ref.shape[0], 2):
            w = jnp.concatenate([w_ref[p, 2 * units :, :], w_ref[p + 1, 2 * units :, :]], axis=1)
            out[first : first + TILE, p * width : (p + 2) * width] = dot(a, w).astype(out.dtype)


def pack_kernel(info, wq, wk, wv, wo, wg, wu, wd, mixer, feed, *outs):
    place = info[0]
    scaled = lambda w, gain: (w[...].astype(F32) * gain[...]).astype(BF16)
    arrays = [scaled(w, mixer) for w in (wq, wk, wv)] + [wo[...]] + [scaled(w, feed) for w in (wg, wu)] + [wd[...]]
    for k, out in enumerate(outs):
        member = place ^ k
        first = 0
        for a in arrays:
            width = a.shape[1] // 4
            best = a[:, :width]
            for q in (1, 2, 3):
                best = jnp.where(member == q, a[:, q * width : (q + 1) * width], best)
            out[:, first : first + width] = best
            first += width


def cut_kernel(first, turn, info, p0, p1, p2, p3, out, whole):
    rows, width = p0.shape[0], whole.shape[1]
    for k, p in enumerate((p0, p1, p2, p3)):
        at = pl.ds(pl.multiple_of((info[0] ^ k) * rows, rows), rows)
        whole[at, :] = p[:, first : first + width].astype(F32)
    a = whole[...]
    out[...] = (a.T if turn else a).astype(BF16)


def cut(info, pieces, first, width, turn, after=(), us=2):
    rows = 4 * pieces[0].shape[0]
    if lax.axis_size("dp") != 8:
        a = in_order(pieces, info[0])[:, first : first + width]
        return a.T if turn else a
    out = shape(width, rows, BF16) if turn else shape(rows, width, BF16)
    return call(
        functools.partial(cut_kernel, first, turn), out, (info,), tuple(pieces), [pltpu.VMEM((rows, width), F32)], after=after, us=us, spare=7 * SPARE
    )


def pack_tokens_kernel(tokens, live, out):
    height = tokens.shape[0]
    out[:height, :] = tokens[...]
    out[height:, :] = jnp.broadcast_to(live[...], out[height:, :].shape).astype(BF16)


def copy_kernel(a, out):
    out[...] = a[...]


def finish_kernel(info, own, t1, t2, t3, e0, e1, e2, e3, whole):
    rows = e0.shape[0] // 3
    units = own.shape[0] // 3
    for n in range(3):
        at = slice(n * units, (n + 1) * units)
        total = own[at, :]
        for t in (t1, t2, t3):
            total = total + t[at, :].astype(F32)
        whole[...] = total.T
        for k, out in enumerate((e0, e1, e2, e3)):
            there = pl.ds(pl.multiple_of((info[0] ^ k) * rows, rows), rows)
            out[n * rows : (n + 1) * rows, :] = whole[there, :].astype(BF16)


def finish(info, place, terms, after=()):
    units, rows = terms[0].shape[0] // 3, terms[0].shape[1]
    if len(terms) == 1:
        blocks = [blocks_of(terms[0][n * units : (n + 1) * units].T.astype(BF16), place) for n in range(3)]
        return [jnp.concatenate([b[k] for b in blocks], axis=0) for k in range(4)]
    return call(
        finish_kernel,
        (shape(3 * rows // 4, units, BF16),) * 4,
        (info,),
        tuple(terms),
        [pltpu.VMEM((rows, units), F32)],
        after=after,
    )


def far_kernel(far, got, out):
    out[...] = (far[...] + got[out.shape[0] :, :].astype(F32)).astype(BF16)


def output_kernel(after, keep, first, got, out):
    out[...] = after[...] + keep[...] + first[: out.shape[0], :].astype(F32) + got[...].astype(F32)


def inputs_kernel(info, back, wa, wb, give, far, keep):
    half = wa.shape[0]
    for k, (out, first) in enumerate(((keep, 0), (give, 0), (far, 0), (give, TILE))):
        a = back[pl.ds(pl.multiple_of((info[0] ^ k) * TILE, TILE), TILE), :]
        out[first : first + TILE, :half] = dot(a, wa[:, : a.shape[1]], NT).astype(out.dtype)
        out[first : first + TILE, half:] = dot(a, wb[:, : a.shape[1]], NT).astype(out.dtype)


def late_middle_kernel(x, back, other, got, own, s1, s2, s3):
    half, width = got.shape[0], back.shape[1]
    rows = half // 4
    one = dot(x[:, :half], back[...], TN) + got[:, :width].astype(F32)
    two = other[...].astype(F32) + got[:, width:].astype(F32)
    own[:, :width] = one[:rows]
    own[:, width:] = two[:rows]
    for k, out in ((1, s1), (2, s2), (3, s3)):
        out[:, :width] = one[k * rows : (k + 1) * rows].astype(BF16)
        out[:, width:] = two[k * rows : (k + 1) * rows].astype(BF16)


def late_middle(x, back, other, give, after):
    half, cols = x.shape[1] // 2, back.shape[1] + other.shape[1]
    if lax.axis_size("dp") != 8:
        keep = jnp.concatenate([dot(x[:, :half], back, TN), other.astype(F32)], axis=1)
        whole = jnp.concatenate([keep, give.astype(F32)], axis=0)
        return [lax.psum_scatter(whole, "dp", scatter_dimension=0, tiled=True)]
    own, *sends = call(
        late_middle_kernel,
        (shape(half // 4, cols, F32),) + (shape(half // 4, cols, BF16),) * 3,
        (),
        (x, back, other, swap(give, "dp", 1)),
        after=after,
    )
    return [own] + [swap(sends[k - 1], "dp", 2 * k) for k in (1, 2, 3)]


def body(
    tokens,
    offsets,
    live_tokens,
    gain_mixer,
    query_weight,
    key_weight,
    value_weight,
    output_weight,
    gain_feed,
    gate_weight,
    up_weight,
    down_weight,
    cotangent,
):
    team = lax.axis_size("fsdp")
    place = lax.axis_index("fsdp")
    height, model = tokens.shape
    length = height * team
    units = gate_weight.shape[1] // team
    kq, kv, ko = (w.shape[1] // team for w in (query_weight, value_weight, output_weight))
    width = 2 * kq + kv
    own_rows = gain_mixer.shape[0]
    slots, blocks = layout()
    info = jnp.concatenate([jnp.full((8,), place, jnp.int32), slots, blocks])

    mixer_col = gain_mixer.astype(F32)[:, None]
    feed_col = gain_feed.astype(F32)[:, None]
    packs = call(
        pack_kernel,
        (shape(own_rows, width + ko + 3 * units, BF16),) * 4,
        (info,),
        (query_weight, key_weight, value_weight, output_weight, gate_weight, up_weight, down_weight, mixer_col, feed_col),
        spare=7 * SPARE,
    )
    packs = exchange(packs)
    first = cut(info, packs, 0, width + ko, False, us=2)
    wa, wb = gather(first, 0)
    feed_w = lax.all_gather(cut(info, packs, width + ko, 3 * units, True, after=(first,), us=2), "dp", axis=0)
    live_row = jnp.pad(live_tokens.astype(F32)[None, :], ((0, 0), (0, model - height)))
    packed = team_pieces(
        call(pack_tokens_kernel, shape(height + 16, model, BF16), (), (tokens, live_row), after=tuple(packs[1:]), us=2)
    )
    straight = call(functools.partial(straight_kernel, width), shape(model, ko, BF16), (info,), (wa, wb), us=2)
    xp, raw, mixed, exact, den, scale_one, row = attend(info, offsets, packed, wa, wb, width, after=(straight,))
    outs = team_pieces(straight)
    wo = call(whole_kernel, shape(model, model, BF16), (info,), tuple(outs), us=3)

    mixes = team_pieces(mixed)
    cots = team_pieces(call(copy_kernel, shape(height, model, BF16), (), (cotangent,), after=(packed[2],)))
    hidden, after, scale_two = call(
        mix_kernel,
        (shape(length, model, BF16), shape(height, model, F32), shape(height, LANES, F32)),
        (info,),
        (*packed, *mixes, wo),
        [pltpu.VMEM((length, model), BF16)], us=7)

    act, turned, give, far, keep = feed(hidden, cots, feed_w)
    got = swap(give, "fsdp", 1)
    far = call(far_kernel, shape(height, model, BF16), (), (far, got))
    give_f, keep_f = feed_grad(info, (0, 1, 2), hidden, cots, turned, after=(far,))
    grad_after, low = call(
        after_kernel,
        (shape(height, model, F32), shape(height, model, BF16)),
        (),
        (keep, got, swap(far, "fsdp", 2), after, scale_two, cotangent),
        after=(give_f,),
    )
    grads = team_pieces(low)

    give2, far2, keep2 = call(
        result_kernel,
        (shape(2 * height, model, BF16), shape(height, model, F32), shape(height, model, F32)),
        (),
        (act, feed_w),
        after=(low,),
    )
    got2 = swap(give2, "fsdp", 1)
    far2 = call(far_kernel, shape(height, model, BF16), (), (far2, got2))
    far_got2 = swap(far2, "fsdp", 2)

    qkv_back, give_l, out_part = attend_back(info, offsets, raw, grads, wo, exact, den, row, scale_one, xp, mixes, after=(far2,))

    give1, far1, keep1 = call(
        inputs_kernel,
        (shape(2 * height, model, BF16), shape(height, model, F32), shape(height, model, F32)),
        (info,),
        (qkv_back, wa, wb),
    )
    got1 = swap(give1, "fsdp", 1)
    far1 = call(far_kernel, shape(height, model, BF16), (), (far1, got1))
    terms_f = middle(give_f, keep_f, after=(far1,))
    terms_l = late_middle(xp, qkv_back, out_part, give_l, after=(terms_f[0],))
    tokens_grad = call(
        tokens_kernel,
        shape(height, model, F32),
        (info,),
        (keep1, got1, swap(far1, "fsdp", 2), scale_one, packed[0], grad_after),
        [pltpu.VMEM((height, model), F32)],
        after=(terms_l[0],),
    )
    output = call(
        output_kernel,
        shape(height, model, F32),
        (),
        (after, keep2, got2, far_got2),
        after=(tokens_grad,),
    )
    feed_pieces = finish(info, place, terms_f, (output,))
    def spread(pieces):
        near = jnp.where(place % 2 == 0, jnp.stack(pieces[:2]), jnp.stack(pieces[1::-1]))
        away = jnp.where(place % 2 == 0, jnp.stack(pieces[2:]), jnp.stack(pieces[:1:-1]))
        whole = jnp.where(place // 2 == 0, jnp.concatenate([near, away], 0), jnp.concatenate([away, near], 0))
        return lambda r, a, b: jnp.concatenate([whole[k, r : r + own_rows, a:b] for k in range(team)], axis=1).astype(F32)

    over = lambda w, g: jnp.sum(w.astype(F32) * g, axis=1)
    wide = spread(exchange(feed_pieces))
    gate_sum, up_sum, down_grad = wide(0, 0, units), wide(own_rows, 0, units), wide(2 * own_rows, 0, units)
    gain_feed_grad = over(gate_weight, gate_sum) + over(up_weight, up_sum)
    gate_grad, up_grad = gate_sum * feed_col, up_sum * feed_col
    late = sum_terms(terms_l, after=(gain_feed_grad, gate_grad, up_grad, down_grad))
    late = spread(exchange(blocks_of(late.astype(BF16), place)))
    q_sum, k_sum, v_sum = late(0, 0, kq), late(0, kq, 2 * kq), late(0, 2 * kq, width)
    out_grad = late(0, width, width + ko)
    gain_mixer_grad = over(query_weight, q_sum) + over(key_weight, k_sum) + over(value_weight, v_sum)
    return (
        output,
        tokens_grad,
        gain_mixer_grad,
        q_sum * mixer_col,
        k_sum * mixer_col,
        v_sum * mixer_col,
        out_grad,
        gain_feed_grad,
        gate_grad,
        up_grad,
        down_grad,
    )


def solution(mesh):
    rows = P(("dp", "fsdp"), None)
    flat = P(("dp", "fsdp"))
    return jax.shard_map(
        body,
        mesh=mesh,
        in_specs=(rows, P("dp", None), flat, flat, rows, rows, rows, rows, flat, rows, rows, rows, rows),
        out_specs=(rows, rows, flat, rows, rows, rows, rows, flat, rows, rows, rows),
        check_vma=False,
    )
```

```python
import functools
import math

import jax
import jax.numpy as jnp
from jax import lax
from jax.experimental import pallas as pl
from jax.experimental.pallas import tpu as pltpu
from jax.sharding import PartitionSpec as P

FDIM = 16
VDIM = 64
EPS = 1e-05
TILE = 256
LANES = 128
SPARE = 8 * 1024 * 1024
SPLIT = 1024

F32 = jnp.float32
BF16 = jnp.bfloat16
NT = ((1,), (1,))
TN = ((0,), (0,))


def dot(a, b, dims=((1,), (0,))):
    return lax.dot_general(a, b, (dims, ((), ())), preferred_element_type=F32)


def shape(rows, cols, dtype):
    return jax.ShapeDtypeStruct((rows, cols), dtype)


def padded(dims, dtype):
    rows, cols = dims[-2:]
    return math.prod(dims[:-2]) * (rows + -rows % 16) * (cols + -cols % LANES) * jnp.dtype(dtype).itemsize


def call(kernel, outs, scalars, arrays, scratch=(), after=(), us=4, spare=SPARE):
    used = len(scalars) + len(arrays)

    def run(*refs):
        kernel(*refs[:used], *refs[used + len(after) :])

    smem = pl.BlockSpec(memory_space=pltpu.SMEM)
    vmem = pl.BlockSpec(memory_space=pltpu.VMEM)
    anywhere = pl.BlockSpec(memory_space=pl.ANY)
    held = sum(padded(a.shape, a.dtype) for a in (*arrays, *jax.tree.leaves(outs), *scratch))
    return pl.pallas_call(
        run,
        out_shape=outs,
        in_specs=[smem] * len(scalars) + [vmem] * len(arrays) + [anywhere] * len(after),
        out_specs=jax.tree.map(lambda _: vmem, outs),
        scratch_shapes=list(scratch),
        compiler_params=pltpu.CompilerParams(vmem_limit_bytes=held + spare),
        cost_estimate=pl.CostEstimate(flops=1, bytes_accessed=us * 3_000_000, transcendentals=0),
    )(*scalars, *arrays, *after)


def swap(a, axis, bit):
    n = lax.axis_size(axis)
    return lax.ppermute(a, axis, [(i, i ^ bit) for i in range(n)])


def part(a, start, size):
    return lax.dynamic_slice_in_dim(a, start, size, 0)


def pick(flag, one, two):
    return jnp.where(flag == 0, jnp.concatenate([one, two], 0), jnp.concatenate([two, one], 0))


def team_pieces(a):
    far = swap(a, "fsdp", 2)
    return a, swap(a, "fsdp", 1), far, swap(far, "fsdp", 1)


def blocks_of(a, place):
    rows = a.shape[0] // 4
    return [part(a, (place ^ k) * rows, rows) for k in range(4)]


def exchange(blocks):
    return [blocks[0]] + [swap(blocks[k], "fsdp", k) for k in (1, 2, 3)]


def in_order(pieces, place):
    high, low = place // 2, place % 2
    return pick(high, pick(low, pieces[0], pieces[1]), pick(low, pieces[2], pieces[3]))


def layout():
    block = jnp.arange(8, dtype=jnp.int32)
    if lax.axis_size("dp") != 8:
        return block, block
    at = lax.axis_index("dp")
    z, y = at // 2, at % 2
    return ((block % 2) ^ y) * 4 + ((block // 2) ^ z), 2 * ((block % 4) ^ z) + ((block // 4) ^ y)


def gather(a, axis):
    if lax.axis_size("dp") != 8:
        whole = lax.all_gather(a, "dp", axis=axis, tiled=True)
        half = whole.shape[axis] // 2
        return lax.slice_in_dim(whole, 0, half, axis=axis), lax.slice_in_dim(whole, half, 2 * half, axis=axis)
    mine = jnp.concatenate([a] + [swap(a, "dp", 2 * k) for k in (1, 2, 3)], axis)
    return mine, swap(mine, "dp", 1)


def lane_of(dims):
    return lax.broadcasted_iota(jnp.int32, dims, len(dims) - 1)


def query_cols(both):
    high = both.astype(BF16).astype(F32)
    low = both - high
    left = lane_of(both.shape) < 64
    one = jnp.where(left, high, pltpu.roll(low, 64, 1))
    two = jnp.where(left, high, 0.0)
    return jnp.concatenate([one.astype(BF16), two.astype(BF16)], axis=1)


def key_cols(both):
    high = both.astype(BF16).astype(F32)
    low = both - high
    left = lane_of(both.shape) < 64
    one = jnp.where(left, pltpu.roll(high, 64, 1), high)
    two = jnp.where(left, pltpu.roll(low, 64, 1), 0.0)
    return jnp.concatenate([one.astype(BF16), two.astype(BF16)], axis=1)


def head_only(a, h, width):
    lane = lane_of(a.shape)
    if width == FDIM:
        lane = lane % 64
    return jnp.where(lane // width == h, a, jnp.zeros_like(a))


def doc_starts(offsets_ref, i):
    place = i * TILE + lax.broadcasted_iota(jnp.int32, (TILE, 1), 0)
    start = jnp.zeros((TILE, 1), jnp.int32)
    for d in range(offsets_ref.shape[1]):
        first = offsets_ref[0, d]
        start = jnp.where(first <= place, jnp.maximum(start, first), start)
    return start


def allowed(start, row, i, j):
    ok = row >= start
    if i == j:
        place = i * TILE + lax.broadcasted_iota(jnp.int32, (TILE, TILE), 0)
        ok = ok & (row <= place)
    return ok


def forward_kernel(info, offsets_ref, t0, t1, t2, t3, wa, wb, xp, raw_ref, mixed_ref, exact_ref, den_ref, scale_ref, row_ref, qc, kc, vc):
    place = info[0]
    blocks = xp.shape[0] // TILE
    half = wa.shape[0]
    team_heads = vc.shape[1] // VDIM
    for k, t in enumerate((t0, t1, t2, t3)):
        block = place ^ k
        at = pl.ds(pl.multiple_of(block * TILE, TILE), TILE)
        x = t[:TILE, :]
        for p in range(8):
            xp[at, pl.ds(pl.multiple_of(info[8 + p] * LANES, LANES), LANES)] = x[:, p * LANES : (p + 1) * LANES]
        live = t[TILE : TILE + 16, :TILE].astype(F32)[:1, :]
        place_row = block * TILE + lane_of((1, TILE))
        row_ref[block] = jnp.broadcast_to(jnp.where(live > 0.5, place_row, -1), (8, TILE))
    for i in range(blocks):
        at = pl.ds(i * TILE, TILE)
        x = xp[at, :]
        wide = x.astype(F32)
        scale = lax.rsqrt(jnp.mean(wide * wide, axis=1, keepdims=True) + EPS)
        scale_ref[at, :] = jnp.broadcast_to(scale, (TILE, LANES))
        raw = (dot(x[:, :half], wa[:, : raw_ref.shape[1]]) + dot(x[:, half:], wb[:, : raw_ref.shape[1]])) * scale
        raw_ref[at, :] = raw
        both = raw[:, :LANES]
        qc[at, :] = query_cols(both)
        kc[at, :] = key_cols(both)
        vc[at, :] = raw[:, LANES:].astype(BF16)
    for i in range(blocks):
        at = pl.ds(i * TILE, TILE)
        start = doc_starts(offsets_ref, i)
        q = qc[at, :]
        result = jnp.zeros((TILE, vc.shape[1]), F32)
        dens = jnp.zeros((TILE, LANES), F32)
        for h in range(team_heads):
            total = jnp.zeros((TILE, vc.shape[1]), F32)
            den = jnp.zeros((TILE, 1), F32)
            for j in range(i + 1):
                there = pl.ds(j * TILE, TILE)
                s = dot(q, head_only(kc[there, :], h, FDIM), NT)
                kept = 1.0 + s * (0.25 + s * 0.03125)
                kept = jnp.where(allowed(start, row_ref[j][:1, :], i, j), kept, 0.0)
                den = den + jnp.sum(kept, axis=1, keepdims=True)
                total = total + dot(kept.astype(BF16), vc[there, :])
            result = jnp.where(lane_of(result.shape) // VDIM == h, total / den, result)
            dens = jnp.where(lane_of(dens.shape) == h, den, dens)
        exact_ref[at, :] = result
        mixed_ref[at, :] = result.astype(BF16)
        den_ref[at, :] = dens


def attend(info, offsets, tokens, wa, wb, width, after=()):
    length = 4 * TILE
    value = width - LANES
    model = tokens[0].shape[1]
    return call(
        forward_kernel,
        (
            shape(length, model, BF16),
            shape(length, width, F32),
            shape(length, value, BF16),
            shape(length, value, F32),
            shape(length, LANES, F32),
            shape(length, LANES, F32),
            jax.ShapeDtypeStruct((4, 8, TILE), jnp.int32),
        ),
        (info, offsets),
        (*tokens, wa, wb),
        [pltpu.VMEM((length, 256), BF16), pltpu.VMEM((length, 256), BF16), pltpu.VMEM((length, value), BF16)], after=after, us=9)


def backward_kernel(info, offsets_ref, raw_ref, g0, g1, g2, g3, wo, exact_ref, den_ref, row_ref, scale_ref, xp, m0, m1, m2, m3, back_ref, give_ref, keep_ref, gm, other, qc, kc, qr, kr, vc, acc):
    place = info[0]
    blocks = raw_ref.shape[0] // TILE
    team_heads = vc.shape[1] // VDIM
    mine_rows = pl.ds(pl.multiple_of(place * TILE, TILE), TILE)
    for k, g in enumerate((g0, g1, g2, g3)):
        at = pl.ds(pl.multiple_of((place ^ k) * TILE, TILE), TILE)
        gm[at, :] = dot(g[...], wo[mine_rows, :], NT)
    for i in range(blocks):
        at = pl.ds(i * TILE, TILE)
        raw = raw_ref[at, :]
        both = raw[:, :LANES]
        qc[at, :] = query_cols(both)
        kc[at, :] = key_cols(both)
        turned = pltpu.roll(both, 64, 1)
        left = lane_of(both.shape) < 64
        kr[at, :] = jnp.where(left, turned, 0.0).astype(BF16)
        qr[at, :] = jnp.where(left, 0.0, turned).astype(BF16)
        vc[at, :] = raw[:, LANES:].astype(BF16)
    acc[...] = jnp.zeros_like(acc)
    for i in range(blocks):
        at = pl.ds(i * TILE, TILE)
        start = doc_starts(offsets_ref, i)
        q = qc[at, :]
        grad = gm[at, :]
        product = grad * exact_ref[at, :]
        dens = den_ref[at, :]
        for h in range(team_heads):
            inverse = 1.0 / jnp.sum(jnp.where(lane_of(dens.shape) == h, dens, 0.0), axis=1, keepdims=True)
            numer = head_only(grad * inverse, h, VDIM).astype(BF16)
            denom = -jnp.sum(head_only(product, h, VDIM), axis=1, keepdims=True) * inverse
            mine = head_only(qr[at, :], h, FDIM)
            back = jnp.zeros((TILE, LANES), F32)
            for j in range(i + 1):
                there = pl.ds(j * TILE, TILE)
                s = dot(q, head_only(kc[there, :], h, FDIM), NT)
                ok = allowed(start, row_ref[j][:1, :], i, j)
                kept = jnp.where(ok, 1.0 + s * (0.25 + s * 0.03125), 0.0)
                inner = dot(numer, vc[there, :], NT) + denom
                inner = jnp.where(ok, inner * (0.25 + s * 0.0625), 0.0).astype(BF16)
                back = back + dot(inner, head_only(kr[there, :], h, FDIM))
                acc[there, :LANES] += dot(inner, mine, TN)
                acc[there, LANES:] += dot(kept.astype(BF16), numer, TN)
            acc[at, :LANES] += back
    for i in range(blocks):
        at = pl.ds(i * TILE, TILE)
        back_ref[at, :] = (acc[at, :] * scale_ref[at, :1]).astype(BF16)
    mine = pl.ds(pl.multiple_of(place * TILE, TILE), TILE)
    for k, m in enumerate((m0, m1, m2, m3)):
        total = jnp.zeros((m.shape[1], TILE), F32)
        for b, g in enumerate((g0, g1, g2, g3)):
            rows = pl.ds(pl.multiple_of((place ^ b) * TILE, TILE), TILE)
            total = total + dot(m[rows, :], g[:, mine], TN)
        for side in (0, 1):
            spot = info[8 + 2 * (place ^ k) + side]
            other[pl.ds(pl.multiple_of(spot * LANES, LANES), LANES), :] = total[side * LANES : (side + 1) * LANES].astype(BF16)
    half, width = give_ref.shape[0], back_ref.shape[1]
    give_ref[:, :width] = dot(xp[:, half:], back_ref[...], TN).astype(BF16)
    give_ref[:, width:] = other[half:, :]
    keep_ref[...] = other[:half, :]


def attend_back(info, offsets, raw, grads, wo, exact, den, row, scale, xp, mixes, after=()):
    length, width = raw.shape
    model, cols = xp.shape[1], grads[0].shape[1] // 4
    value = width - LANES
    return call(
        backward_kernel,
        (
            shape(length, width, BF16),
            shape(model // 2, width + cols, BF16),
            shape(model // 2, cols, BF16),
        ),
        (info, offsets),
        (raw, *grads, wo, exact, den, row, scale, xp, *mixes),
        [
            pltpu.VMEM((length, value), F32),
            pltpu.VMEM((model, cols), BF16),
            pltpu.VMEM((length, 256), BF16),
            pltpu.VMEM((length, 256), BF16),
            pltpu.VMEM((length, LANES), BF16),
            pltpu.VMEM((length, LANES), BF16),
            pltpu.VMEM((length, value), BF16),
            pltpu.VMEM((length, width), F32),
        ],
        after=after, us=18)


def straight_kernel(cols, info, a, b, out):
    for n in range(8):
        source, first = (a, n * LANES) if n < 4 else (b, (n - 4) * LANES)
        out[pl.ds(pl.multiple_of(info[16 + n] * LANES, LANES), LANES), :] = source[first : first + LANES, cols:]


def whole_kernel(info, o0, o1, o2, o3, out):
    for k, o in enumerate((o0, o1, o2, o3)):
        out[:, pl.ds(pl.multiple_of((info[0] ^ k) * TILE, TILE), TILE)] = o[...]


def mix_kernel(info, t0, t1, t2, t3, m0, m1, m2, m3, wo, hidden_ref, own_ref, scale_ref, mixed):
    place = info[0]
    for k, m in enumerate((m0, m1, m2, m3)):
        mixed[:, pl.ds(pl.multiple_of((place ^ k) * TILE, TILE), TILE)] = m[...]
    for k, t in enumerate((t0, t1, t2, t3)):
        rows = pl.ds(pl.multiple_of((place ^ k) * TILE, TILE), TILE)
        total = t[:TILE, :].astype(F32) + dot(mixed[rows, :], wo[...])
        scale = lax.rsqrt(jnp.mean(total * total, axis=1, keepdims=True) + EPS)
        hidden_ref[k * TILE : (k + 1) * TILE, :] = (total * scale).astype(BF16)
        if k == 0:
            own_ref[...] = total
            scale_ref[...] = jnp.broadcast_to(scale, scale_ref.shape)


def feed_kernel(hidden_ref, c0, c1, c2, c3, w_ref, act_ref, turned_ref, give, far, keep, w):
    units = w.shape[0] // 3
    for p in range(w_ref.shape[0]):
        width = w_ref.shape[2]
        w[:, p * width : (p + 1) * width] = w_ref[p]
    gw, uw, dw = (w[n * units : (n + 1) * units, :] for n in range(3))
    outs = ((keep, 0), (give, 0), (far, 0), (give, TILE))
    for k, c in enumerate((c0, c1, c2, c3)):
        at = slice(k * TILE, (k + 1) * TILE)
        h = hidden_ref[at, :]
        gate = dot(h, gw, NT)
        lift = dot(h, uw, NT)
        grad = dot(c[...], dw, NT)
        sig = 1.0 / (1.0 + jnp.exp(-gate))
        silu = gate * sig
        act = (silu * lift).astype(BF16)
        gate_back = (grad * lift * (sig + silu * (1.0 - sig))).astype(BF16)
        lift_back = (grad * silu).astype(BF16)
        act_ref[at, :] = act
        out, first = outs[k]
        out[first : first + TILE, :] = (dot(gate_back, gw) + dot(lift_back, uw)).astype(out.dtype)
        turned_ref[:units, at] = gate_back.T
        turned_ref[units : 2 * units, at] = lift_back.T
        turned_ref[2 * units :, at] = act.T


def feed(hidden, cots, weights):
    rows, model = hidden.shape
    units = weights.shape[1] // 3
    return call(
        feed_kernel,
        (
            shape(rows, units, BF16),
            shape(3 * units, rows, BF16),
            shape(rows // 2, model, BF16),
            shape(rows // 4, model, F32),
            shape(rows // 4, model, F32),
        ),
        (),
        (hidden, *cots, weights),
        [pltpu.VMEM((3 * units, model), BF16)], us=15)


def feed_grad_kernel(first, info, hidden, *refs):
    cots, (turned, give, keep, whole) = refs[:-4], refs[-4:]
    split = 2 * (turned.shape[0] // 3)
    last = first + give.shape[0]
    width = hidden.shape[1] // 8
    half = hidden.shape[1] // 2
    for start, end in ((first, min(last, split)), (max(first, split), last)):
        if start >= end:
            continue
        if start < split:
            total = dot(turned[start:end, :], hidden[...])
        else:
            total = sum(dot(turned[start:end, k * TILE : (k + 1) * TILE], c[...]) for k, c in enumerate(cots))
        out = slice(start - first, end - first)
        for p in range(8):
            spot = pl.ds(pl.multiple_of(info[8 + p] * width, width), width)
            whole[out, spot] = total[:, p * width : (p + 1) * width].astype(BF16)
    keep[...] = whole[:, :half]
    give[...] = whole[:, half:]


def feed_grad(info, first, rows, hidden, cots, turned, after=()):
    model = hidden.shape[1]
    return call(
        functools.partial(feed_grad_kernel, first),
        (shape(rows, model // 2, BF16),) * 2,
        (info,),
        (hidden, *cots, turned),
        [pltpu.VMEM((rows, model), BF16)],
        after=after,
    )


def middle_kernel(keep, got, own, *sends):
    size = own.shape[1]
    own[...] = keep[:, :size].astype(F32) + got[:, :size].astype(F32)
    for k in (1, 2, 3):
        cols = slice(k * size, (k + 1) * size)
        sends[k - 1][...] = (keep[:, cols].astype(F32) + got[:, cols].astype(F32)).astype(BF16)


def middle(give, keep, after=()):
    units, half = keep.shape
    if lax.axis_size("dp") != 8:
        whole = jnp.concatenate([keep, give], axis=1).astype(F32)
        return [lax.psum_scatter(whole, "dp", scatter_dimension=1, tiled=True)]
    outs = (shape(units, half // 4, F32),) + (shape(units, half // 4, BF16),) * 3
    own, *sends = call(middle_kernel, outs, (), (keep, swap(give, "dp", 1)), after=after)
    return [own] + [swap(sends[k - 1], "dp", 2 * k) for k in (1, 2, 3)]


def sum_kernel(*refs):
    total = refs[0][...]
    for t in refs[1:-1]:
        total = total + t[...].astype(F32)
    refs[-1][...] = total


def sum_terms(terms, after=()):
    if len(terms) == 1:
        return terms[0]
    return call(sum_kernel, shape(*terms[0].shape, F32), (), tuple(terms), after=after)


def after_kernel(keep, first, got, after_ref, scale_ref, cot, grad_ref, low_ref):
    total = keep[...] + first[:TILE, :].astype(F32) + got[...].astype(F32)
    after = after_ref[...]
    scale = scale_ref[:, :1]
    inner = jnp.mean(after * total, axis=1, keepdims=True)
    grad = cot[...].astype(F32) + scale * total - after * (scale * scale * scale * inner)
    grad_ref[...] = grad
    low_ref[...] = grad.astype(BF16)


def tokens_kernel(info, keep, first, got, scale_ref, tokens, grad, out, straight):
    for p in range(8):
        spot = pl.ds(pl.multiple_of(info[8 + p] * LANES, LANES), LANES)
        straight[:, p * LANES : (p + 1) * LANES] = keep[:, spot] + first[:TILE, spot].astype(F32) + got[:, spot].astype(F32)
    total = straight[...]
    x = tokens[:TILE, :].astype(F32)
    scale = scale_ref[pl.ds(pl.multiple_of(info[0] * TILE, TILE), TILE), :][:, :1]
    out[...] = grad[...] + total - x * (scale * scale * jnp.mean(x * total, axis=1, keepdims=True))


def result_kernel(act, w_ref, give, far, keep):
    units = act.shape[1]
    width = w_ref.shape[2]
    for k, (out, first) in enumerate(((keep, 0), (give, 0), (far, 0), (give, TILE))):
        a = act[k * TILE : (k + 1) * TILE, :]
        for p in range(0, w_ref.shape[0], 2):
            w = jnp.concatenate([w_ref[p, 2 * units :, :], w_ref[p + 1, 2 * units :, :]], axis=1)
            out[first : first + TILE, p * width : (p + 2) * width] = dot(a, w).astype(out.dtype)


def pack_kernel(info, wq, wk, wv, wo, wg, wu, wd, mixer, feed, *outs):
    place = info[0]
    scaled = lambda w, gain: (w[...].astype(F32) * gain[...]).astype(BF16)
    arrays = [scaled(w, mixer) for w in (wq, wk, wv)] + [wo[...]] + [scaled(w, feed) for w in (wg, wu)] + [wd[...]]
    for k, out in enumerate(outs):
        member = place ^ k
        first = 0
        for a in arrays:
            width = a.shape[1] // 4
            best = a[:, :width]
            for q in (1, 2, 3):
                best = jnp.where(member == q, a[:, q * width : (q + 1) * width], best)
            out[:, first : first + width] = best
            first += width


def cut_kernel(first, turn, info, p0, p1, p2, p3, out, whole):
    rows, width = p0.shape[0], whole.shape[1]
    for k, p in enumerate((p0, p1, p2, p3)):
        at = pl.ds(pl.multiple_of((info[0] ^ k) * rows, rows), rows)
        whole[at, :] = p[:, first : first + width].astype(F32)
    a = whole[...]
    out[...] = (a.T if turn else a).astype(BF16)


def cut(info, pieces, first, width, turn, after=(), us=2):
    rows = 4 * pieces[0].shape[0]
    if lax.axis_size("dp") != 8:
        a = in_order(pieces, info[0])[:, first : first + width]
        return a.T if turn else a
    out = shape(width, rows, BF16) if turn else shape(rows, width, BF16)
    return call(
        functools.partial(cut_kernel, first, turn), out, (info,), tuple(pieces), [pltpu.VMEM((rows, width), F32)], after=after, us=us, spare=7 * SPARE
    )


def pack_tokens_kernel(tokens, live, out):
    height = tokens.shape[0]
    out[:height, :] = tokens[...]
    out[height:, :] = jnp.broadcast_to(live[...], out[height:, :].shape).astype(BF16)


def copy_kernel(a, out):
    out[...] = a[...]


def finish_kernel(info, summed, own, t1, t2, t3, e0, e1, e2, e3, turned, whole):
    rows = e0.shape[0] // 3
    chunk = own.shape[0]
    total = own[...]
    for t in (t1, t2, t3):
        total = total + t[...].astype(F32)
    turned[:chunk, :] = total
    turned[chunk:, :] = summed[...]
    units = turned.shape[0] // 3
    for n in range(3):
        whole[...] = turned[n * units : (n + 1) * units, :].T
        for k, out in enumerate((e0, e1, e2, e3)):
            there = pl.ds(pl.multiple_of((info[0] ^ k) * rows, rows), rows)
            out[n * rows : (n + 1) * rows, :] = whole[there, :].astype(BF16)


def finish(info, place, summed, terms, after=()):
    height, rows = summed.shape[0] + terms[0].shape[0], summed.shape[1]
    units = height // 3
    if len(terms) == 1:
        both = jnp.concatenate([terms[0], summed], axis=0)
        blocks = [blocks_of(both[n * units : (n + 1) * units].T.astype(BF16), place) for n in range(3)]
        return [jnp.concatenate([b[k] for b in blocks], axis=0) for k in range(4)]
    return call(
        finish_kernel,
        (shape(3 * rows // 4, units, BF16),) * 4,
        (info,),
        (summed, *terms),
        [pltpu.VMEM((height, rows), F32), pltpu.VMEM((rows, units), F32)],
        after=after,
    )


def far_kernel(far, got, out):
    out[...] = (far[...] + got[out.shape[0] :, :].astype(F32)).astype(BF16)


def output_kernel(after, keep, first, got, out):
    out[...] = after[...] + keep[...] + first[: out.shape[0], :].astype(F32) + got[...].astype(F32)


def inputs_kernel(info, back, wa, wb, give, far, keep):
    half = wa.shape[0]
    for k, (out, first) in enumerate(((keep, 0), (give, 0), (far, 0), (give, TILE))):
        a = back[pl.ds(pl.multiple_of((info[0] ^ k) * TILE, TILE), TILE), :]
        out[first : first + TILE, :half] = dot(a, wa[:, : a.shape[1]], NT).astype(out.dtype)
        out[first : first + TILE, half:] = dot(a, wb[:, : a.shape[1]], NT).astype(out.dtype)


def late_middle_kernel(x, back, other, got, own, s1, s2, s3):
    half, width = got.shape[0], back.shape[1]
    rows = half // 4
    one = dot(x[:, :half], back[...], TN) + got[:, :width].astype(F32)
    two = other[...].astype(F32) + got[:, width:].astype(F32)
    own[:, :width] = one[:rows]
    own[:, width:] = two[:rows]
    for k, out in ((1, s1), (2, s2), (3, s3)):
        out[:, :width] = one[k * rows : (k + 1) * rows].astype(BF16)
        out[:, width:] = two[k * rows : (k + 1) * rows].astype(BF16)


def late_middle(x, back, other, give, after):
    half, cols = x.shape[1] // 2, back.shape[1] + other.shape[1]
    if lax.axis_size("dp") != 8:
        keep = jnp.concatenate([dot(x[:, :half], back, TN), other.astype(F32)], axis=1)
        whole = jnp.concatenate([keep, give.astype(F32)], axis=0)
        return [lax.psum_scatter(whole, "dp", scatter_dimension=0, tiled=True)]
    own, *sends = call(
        late_middle_kernel,
        (shape(half // 4, cols, F32),) + (shape(half // 4, cols, BF16),) * 3,
        (),
        (x, back, other, swap(give, "dp", 1)),
        after=after,
    )
    return [own] + [swap(sends[k - 1], "dp", 2 * k) for k in (1, 2, 3)]


def body(
    tokens,
    offsets,
    live_tokens,
    gain_mixer,
    query_weight,
    key_weight,
    value_weight,
    output_weight,
    gain_feed,
    gate_weight,
    up_weight,
    down_weight,
    cotangent,
):
    team = lax.axis_size("fsdp")
    place = lax.axis_index("fsdp")
    height, model = tokens.shape
    length = height * team
    units = gate_weight.shape[1] // team
    kq, kv, ko = (w.shape[1] // team for w in (query_weight, value_weight, output_weight))
    width = 2 * kq + kv
    own_rows = gain_mixer.shape[0]
    slots, blocks = layout()
    info = jnp.concatenate([jnp.full((8,), place, jnp.int32), slots, blocks])

    mixer_col = gain_mixer.astype(F32)[:, None]
    feed_col = gain_feed.astype(F32)[:, None]
    packs = call(
        pack_kernel,
        (shape(own_rows, width + ko + 3 * units, BF16),) * 4,
        (info,),
        (query_weight, key_weight, value_weight, output_weight, gate_weight, up_weight, down_weight, mixer_col, feed_col),
        spare=7 * SPARE,
    )
    packs = exchange(packs)
    first = cut(info, packs, 0, width + ko, False, us=2)
    wa, wb = gather(first, 0)
    feed_w = lax.all_gather(cut(info, packs, width + ko, 3 * units, True, after=(first,), us=2), "dp", axis=0)
    live_row = jnp.pad(live_tokens.astype(F32)[None, :], ((0, 0), (0, model - height)))
    packed = team_pieces(
        call(pack_tokens_kernel, shape(height + 16, model, BF16), (), (tokens, live_row), after=tuple(packs[1:]), us=2)
    )
    straight = call(functools.partial(straight_kernel, width), shape(model, ko, BF16), (info,), (wa, wb), us=2)
    xp, raw, mixed, exact, den, scale_one, row = attend(info, offsets, packed, wa, wb, width, after=(straight,))
    outs = team_pieces(straight)
    wo = call(whole_kernel, shape(model, model, BF16), (info,), tuple(outs), us=3)

    mixes = team_pieces(mixed)
    cots = team_pieces(call(copy_kernel, shape(height, model, BF16), (), (cotangent,), after=(packed[2],)))
    hidden, after, scale_two = call(
        mix_kernel,
        (shape(length, model, BF16), shape(height, model, F32), shape(height, LANES, F32)),
        (info,),
        (*packed, *mixes, wo),
        [pltpu.VMEM((length, model), BF16)], us=7)

    act, turned, give, far, keep = feed(hidden, cots, feed_w)
    got = swap(give, "fsdp", 1)
    far = call(far_kernel, shape(height, model, BF16), (), (far, got))
    chunk = SPLIT
    give_b, keep_b = feed_grad(info, chunk, 3 * units - chunk, hidden, cots, turned, after=(far,))
    give_a, keep_a = feed_grad(info, 0, chunk, hidden, (), turned, after=(give_b,))
    grad_after, low = call(
        after_kernel,
        (shape(height, model, F32), shape(height, model, BF16)),
        (),
        (keep, got, swap(far, "fsdp", 2), after, scale_two, cotangent),
        after=(give_a,),
    )
    grads = team_pieces(low)

    terms_b = middle(give_b, keep_b, after=(low,))

    qkv_back, give_l, out_part = attend_back(info, offsets, raw, grads, wo, exact, den, row, scale_one, xp, mixes, after=(terms_b[0],))

    sum_b = sum_terms(terms_b, after=(qkv_back,))
    terms_a = middle(give_a, keep_a, after=(sum_b,))
    give1, far1, keep1 = call(
        inputs_kernel,
        (shape(2 * height, model, BF16), shape(height, model, F32), shape(height, model, F32)),
        (info,),
        (qkv_back, wa, wb),
        after=(terms_a[0],),
    )
    got1 = swap(give1, "fsdp", 1)
    far1 = call(far_kernel, shape(height, model, BF16), (), (far1, got1))
    give2, far2, keep2 = call(
        result_kernel,
        (shape(2 * height, model, BF16), shape(height, model, F32), shape(height, model, F32)),
        (),
        (act, feed_w),
        after=(far1,),
    )
    got2 = swap(give2, "fsdp", 1)
    far2 = call(far_kernel, shape(height, model, BF16), (), (far2, got2))
    far_got2 = swap(far2, "fsdp", 2)
    terms_l = late_middle(xp, qkv_back, out_part, give_l, after=(far2,))
    tokens_grad = call(
        tokens_kernel,
        shape(height, model, F32),
        (info,),
        (keep1, got1, swap(far1, "fsdp", 2), scale_one, packed[0], grad_after),
        [pltpu.VMEM((height, model), F32)],
        after=(terms_l[0],),
    )
    output = call(
        output_kernel,
        shape(height, model, F32),
        (),
        (after, keep2, got2, far_got2),
        after=(tokens_grad,),
    )
    feed_pieces = finish(info, place, sum_b, terms_a, (output,))
    def spread(pieces):
        near = jnp.where(place % 2 == 0, jnp.stack(pieces[:2]), jnp.stack(pieces[1::-1]))
        away = jnp.where(place % 2 == 0, jnp.stack(pieces[2:]), jnp.stack(pieces[:1:-1]))
        whole = jnp.where(place // 2 == 0, jnp.concatenate([near, away], 0), jnp.concatenate([away, near], 0))
        return lambda r, a, b: jnp.concatenate([whole[k, r : r + own_rows, a:b] for k in range(team)], axis=1).astype(F32)

    over = lambda w, g: jnp.sum(w.astype(F32) * g, axis=1)
    wide = spread(exchange(feed_pieces))
    gate_sum, up_sum, down_grad = wide(0, 0, units), wide(own_rows, 0, units), wide(2 * own_rows, 0, units)
    gain_feed_grad = over(gate_weight, gate_sum) + over(up_weight, up_sum)
    gate_grad, up_grad = gate_sum * feed_col, up_sum * feed_col
    late = sum_terms(terms_l, after=(gain_feed_grad, gate_grad, up_grad, down_grad))
    late = spread(exchange(blocks_of(late.astype(BF16), place)))
    q_sum, k_sum, v_sum = late(0, 0, kq), late(0, kq, 2 * kq), late(0, 2 * kq, width)
    out_grad = late(0, width, width + ko)
    gain_mixer_grad = over(query_weight, q_sum) + over(key_weight, k_sum) + over(value_weight, v_sum)
    return (
        output,
        tokens_grad,
        gain_mixer_grad,
        q_sum * mixer_col,
        k_sum * mixer_col,
        v_sum * mixer_col,
        out_grad,
        gain_feed_grad,
        gate_grad,
        up_grad,
        down_grad,
    )


def solution(mesh):
    rows = P(("dp", "fsdp"), None)
    flat = P(("dp", "fsdp"))
    return jax.shard_map(
        body,
        mesh=mesh,
        in_specs=(rows, P("dp", None), flat, flat, rows, rows, rows, rows, flat, rows, rows, rows, rows),
        out_specs=(rows, rows, flat, rows, rows, rows, rows, flat, rows, rows, rows),
        check_vma=False,
    )
```

```python
import functools
import math

import jax
import jax.numpy as jnp
from jax import lax
from jax.experimental import pallas as pl
from jax.experimental.pallas import tpu as pltpu
from jax.sharding import PartitionSpec as P

FDIM = 16
VDIM = 64
EPS = 1e-05
TILE = 256
LANES = 128
SPARE = 8 * 1024 * 1024
SPLIT = 1024

F32 = jnp.float32
BF16 = jnp.bfloat16
NT = ((1,), (1,))
TN = ((0,), (0,))


def dot(a, b, dims=((1,), (0,))):
    return lax.dot_general(a, b, (dims, ((), ())), preferred_element_type=F32)


def shape(rows, cols, dtype):
    return jax.ShapeDtypeStruct((rows, cols), dtype)


def padded(dims, dtype):
    rows, cols = dims[-2:]
    return math.prod(dims[:-2]) * (rows + -rows % 16) * (cols + -cols % LANES) * jnp.dtype(dtype).itemsize


def call(kernel, outs, scalars, arrays, scratch=(), after=(), us=4, spare=SPARE):
    used = len(scalars) + len(arrays)

    def run(*refs):
        kernel(*refs[:used], *refs[used + len(after) :])

    smem = pl.BlockSpec(memory_space=pltpu.SMEM)
    vmem = pl.BlockSpec(memory_space=pltpu.VMEM)
    anywhere = pl.BlockSpec(memory_space=pl.ANY)
    held = sum(padded(a.shape, a.dtype) for a in (*arrays, *jax.tree.leaves(outs), *scratch))
    return pl.pallas_call(
        run,
        out_shape=outs,
        in_specs=[smem] * len(scalars) + [vmem] * len(arrays) + [anywhere] * len(after),
        out_specs=jax.tree.map(lambda _: vmem, outs),
        scratch_shapes=list(scratch),
        compiler_params=pltpu.CompilerParams(vmem_limit_bytes=held + spare),
        cost_estimate=pl.CostEstimate(flops=1, bytes_accessed=us * 3_000_000, transcendentals=0),
    )(*scalars, *arrays, *after)


def swap(a, axis, bit):
    n = lax.axis_size(axis)
    return lax.ppermute(a, axis, [(i, i ^ bit) for i in range(n)])


def part(a, start, size):
    return lax.dynamic_slice_in_dim(a, start, size, 0)


def pick(flag, one, two):
    return jnp.where(flag == 0, jnp.concatenate([one, two], 0), jnp.concatenate([two, one], 0))


def team_pieces(a):
    far = swap(a, "fsdp", 2)
    return a, swap(a, "fsdp", 1), far, swap(far, "fsdp", 1)


def blocks_of(a, place):
    rows = a.shape[0] // 4
    return [part(a, (place ^ k) * rows, rows) for k in range(4)]


def exchange(blocks):
    return [blocks[0]] + [swap(blocks[k], "fsdp", k) for k in (1, 2, 3)]


def in_order(pieces, place):
    high, low = place // 2, place % 2
    return pick(high, pick(low, pieces[0], pieces[1]), pick(low, pieces[2], pieces[3]))


def layout():
    block = jnp.arange(8, dtype=jnp.int32)
    if lax.axis_size("dp") != 8:
        return block, block
    at = lax.axis_index("dp")
    z, y = at // 2, at % 2
    return ((block % 2) ^ y) * 4 + ((block // 2) ^ z), 2 * ((block % 4) ^ z) + ((block // 4) ^ y)


def gather(a, axis):
    if lax.axis_size("dp") != 8:
        whole = lax.all_gather(a, "dp", axis=axis, tiled=True)
        half = whole.shape[axis] // 2
        return lax.slice_in_dim(whole, 0, half, axis=axis), lax.slice_in_dim(whole, half, 2 * half, axis=axis)
    mine = jnp.concatenate([a] + [swap(a, "dp", 2 * k) for k in (1, 2, 3)], axis)
    return mine, swap(mine, "dp", 1)


def lane_of(dims):
    return lax.broadcasted_iota(jnp.int32, dims, len(dims) - 1)


def query_cols(both):
    high = both.astype(BF16).astype(F32)
    low = both - high
    left = lane_of(both.shape) < 64
    one = jnp.where(left, high, pltpu.roll(low, 64, 1))
    two = jnp.where(left, high, 0.0)
    return jnp.concatenate([one.astype(BF16), two.astype(BF16)], axis=1)


def key_cols(both):
    high = both.astype(BF16).astype(F32)
    low = both - high
    left = lane_of(both.shape) < 64
    one = jnp.where(left, pltpu.roll(high, 64, 1), high)
    two = jnp.where(left, pltpu.roll(low, 64, 1), 0.0)
    return jnp.concatenate([one.astype(BF16), two.astype(BF16)], axis=1)


def head_only(a, h, width):
    lane = lane_of(a.shape)
    if width == FDIM:
        lane = lane % 64
    return jnp.where(lane // width == h, a, jnp.zeros_like(a))


def doc_starts(offsets_ref, i):
    place = i * TILE + lax.broadcasted_iota(jnp.int32, (TILE, 1), 0)
    start = jnp.zeros((TILE, 1), jnp.int32)
    for d in range(offsets_ref.shape[1]):
        first = offsets_ref[0, d]
        start = jnp.where(first <= place, jnp.maximum(start, first), start)
    return start


def allowed(start, row, i, j):
    ok = row >= start
    if i == j:
        place = i * TILE + lax.broadcasted_iota(jnp.int32, (TILE, TILE), 0)
        ok = ok & (row <= place)
    return ok


def forward_kernel(info, offsets_ref, t0, t1, t2, t3, wa, wb, xp, raw_ref, mixed_ref, exact_ref, den_ref, scale_ref, row_ref, qc, kc, vc):
    place = info[0]
    blocks = xp.shape[0] // TILE
    half = wa.shape[0]
    team_heads = vc.shape[1] // VDIM
    for k, t in enumerate((t0, t1, t2, t3)):
        block = place ^ k
        at = pl.ds(pl.multiple_of(block * TILE, TILE), TILE)
        x = t[:TILE, :]
        for p in range(8):
            xp[at, pl.ds(pl.multiple_of(info[8 + p] * LANES, LANES), LANES)] = x[:, p * LANES : (p + 1) * LANES]
        live = t[TILE : TILE + 16, :TILE].astype(F32)[:1, :]
        place_row = block * TILE + lane_of((1, TILE))
        row_ref[block] = jnp.broadcast_to(jnp.where(live > 0.5, place_row, -1), (8, TILE))
    for i in range(blocks):
        at = pl.ds(i * TILE, TILE)
        x = xp[at, :]
        wide = x.astype(F32)
        scale = lax.rsqrt(jnp.mean(wide * wide, axis=1, keepdims=True) + EPS)
        scale_ref[at, :] = jnp.broadcast_to(scale, (TILE, LANES))
        raw = (dot(x[:, :half], wa[:, : raw_ref.shape[1]]) + dot(x[:, half:], wb[:, : raw_ref.shape[1]])) * scale
        raw_ref[at, :] = raw
        both = raw[:, :LANES]
        qc[at, :] = query_cols(both)
        kc[at, :] = key_cols(both)
        vc[at, :] = raw[:, LANES:].astype(BF16)
    for i in range(blocks):
        at = pl.ds(i * TILE, TILE)
        start = doc_starts(offsets_ref, i)
        q = qc[at, :]
        result = jnp.zeros((TILE, vc.shape[1]), F32)
        dens = jnp.zeros((TILE, LANES), F32)
        for h in range(team_heads):
            total = jnp.zeros((TILE, vc.shape[1]), F32)
            den = jnp.zeros((TILE, 1), F32)
            qh = head_only(q, h, FDIM)
            for j in range(i + 1):
                there = pl.ds(j * TILE, TILE)
                s = dot(qh, kc[there, :], NT)
                kept = 1.0 + s * (0.25 + s * 0.03125)
                kept = jnp.where(allowed(start, row_ref[j][:1, :], i, j), kept, 0.0)
                den = den + jnp.sum(kept, axis=1, keepdims=True)
                total = total + dot(kept.astype(BF16), vc[there, :])
            result = jnp.where(lane_of(result.shape) // VDIM == h, total / den, result)
            dens = jnp.where(lane_of(dens.shape) == h, den, dens)
        exact_ref[at, :] = result
        mixed_ref[at, :] = result.astype(BF16)
        den_ref[at, :] = dens


def attend(info, offsets, tokens, wa, wb, width, after=()):
    length = 4 * TILE
    value = width - LANES
    model = tokens[0].shape[1]
    return call(
        forward_kernel,
        (
            shape(length, model, BF16),
            shape(length, width, F32),
            shape(length, value, BF16),
            shape(length, value, F32),
            shape(length, LANES, F32),
            shape(length, LANES, F32),
            jax.ShapeDtypeStruct((4, 8, TILE), jnp.int32),
        ),
        (info, offsets),
        (*tokens, wa, wb),
        [pltpu.VMEM((length, 256), BF16), pltpu.VMEM((length, 256), BF16), pltpu.VMEM((length, value), BF16)], after=after, us=9)


def backward_kernel(info, offsets_ref, raw_ref, g0, g1, g2, g3, wo, exact_ref, den_ref, row_ref, scale_ref, xp, m0, m1, m2, m3, back_ref, give_ref, keep_ref, gm, other, qc, kc, qr, kr, vc, acc, over):
    place = info[0]
    blocks = raw_ref.shape[0] // TILE
    team_heads = vc.shape[1] // VDIM
    mine_rows = pl.ds(pl.multiple_of(place * TILE, TILE), TILE)
    for k, g in enumerate((g0, g1, g2, g3)):
        at = pl.ds(pl.multiple_of((place ^ k) * TILE, TILE), TILE)
        gm[at, :] = dot(g[...], wo[mine_rows, :], NT)
    for i in range(blocks):
        at = pl.ds(i * TILE, TILE)
        raw = raw_ref[at, :]
        both = raw[:, :LANES]
        qc[at, :] = query_cols(both)
        kc[at, :] = key_cols(both)
        turned = pltpu.roll(both, 64, 1)
        left = lane_of(both.shape) < 64
        kr[at, :] = jnp.where(left, turned, 0.0).astype(BF16)
        qr[at, :] = jnp.where(left, 0.0, turned).astype(BF16)
        vc[at, :] = raw[:, LANES:].astype(BF16)
    acc[...] = jnp.zeros_like(acc)
    over[...] = jnp.zeros_like(over)
    for i in range(blocks):
        at = pl.ds(i * TILE, TILE)
        start = doc_starts(offsets_ref, i)
        q = qc[at, :]
        grad = gm[at, :]
        product = grad * exact_ref[at, :]
        dens = den_ref[at, :]
        heads = []
        for h in range(team_heads):
            inverse = 1.0 / jnp.sum(jnp.where(lane_of(dens.shape) == h, dens, 0.0), axis=1, keepdims=True)
            numer = head_only(grad * inverse, h, VDIM).astype(BF16)
            denom = -jnp.sum(head_only(product, h, VDIM), axis=1, keepdims=True) * inverse
            mine = qr[at, :].T[64 + h * FDIM : 64 + (h + 1) * FDIM, :]
            heads.append((head_only(q, h, FDIM), numer, denom, mine, numer.T[h * VDIM : (h + 1) * VDIM, :]))
        for j in range(i + 1):
            there = pl.ds(j * TILE, TILE)
            ok = allowed(start, row_ref[j][:1, :], i, j)
            keys = kc[there, :]
            values = vc[there, :]
            straight = kr[there, :]
            back = jnp.zeros((TILE, LANES), F32)
            for h, (qh, numer, denom, mine, tall) in enumerate(heads):
                s = dot(qh, keys, NT)
                kept = jnp.where(ok, 1.0 + s * (0.25 + s * 0.03125), 0.0)
                inner = dot(numer, values, NT) + denom
                inner = jnp.where(ok, inner * (0.25 + s * 0.0625), 0.0).astype(BF16)
                back = back + head_only(dot(inner, straight), h, FDIM)
                keys_rows = slice(64 + h * FDIM, 64 + (h + 1) * FDIM)
                value_rows = slice(LANES + h * VDIM, LANES + (h + 1) * VDIM)
                over[keys_rows, there] += dot(mine, inner)
                over[value_rows, there] += dot(tall, kept.astype(BF16))
            acc[at, :] += back
    for i in range(blocks):
        at = pl.ds(i * TILE, TILE)
        both = over[:, at].T
        scale = scale_ref[at, :1]
        back_ref[at, :LANES] = ((acc[at, :] + both[:, :LANES]) * scale).astype(BF16)
        back_ref[at, LANES:] = (both[:, LANES:] * scale).astype(BF16)
    mine = pl.ds(pl.multiple_of(place * TILE, TILE), TILE)
    for k, m in enumerate((m0, m1, m2, m3)):
        total = jnp.zeros((m.shape[1], TILE), F32)
        for b, g in enumerate((g0, g1, g2, g3)):
            rows = pl.ds(pl.multiple_of((place ^ b) * TILE, TILE), TILE)
            total = total + dot(m[rows, :], g[:, mine], TN)
        for side in (0, 1):
            spot = info[8 + 2 * (place ^ k) + side]
            other[pl.ds(pl.multiple_of(spot * LANES, LANES), LANES), :] = total[side * LANES : (side + 1) * LANES].astype(BF16)
    half, width = give_ref.shape[0], back_ref.shape[1]
    give_ref[:, :width] = dot(xp[:, half:], back_ref[...], TN).astype(BF16)
    give_ref[:, width:] = other[half:, :]
    keep_ref[...] = other[:half, :]


def attend_back(info, offsets, raw, grads, wo, exact, den, row, scale, xp, mixes, after=()):
    length, width = raw.shape
    model, cols = xp.shape[1], grads[0].shape[1] // 4
    value = width - LANES
    return call(
        backward_kernel,
        (
            shape(length, width, BF16),
            shape(model // 2, width + cols, BF16),
            shape(model // 2, cols, BF16),
        ),
        (info, offsets),
        (raw, *grads, wo, exact, den, row, scale, xp, *mixes),
        [
            pltpu.VMEM((length, value), F32),
            pltpu.VMEM((model, cols), BF16),
            pltpu.VMEM((length, 256), BF16),
            pltpu.VMEM((length, 256), BF16),
            pltpu.VMEM((length, LANES), BF16),
            pltpu.VMEM((length, LANES), BF16),
            pltpu.VMEM((length, value), BF16),
            pltpu.VMEM((length, LANES), F32),
            pltpu.VMEM((width, length), F32),
        ],
        after=after, us=18)


def straight_kernel(cols, info, a, b, out):
    for n in range(8):
        source, first = (a, n * LANES) if n < 4 else (b, (n - 4) * LANES)
        out[pl.ds(pl.multiple_of(info[16 + n] * LANES, LANES), LANES), :] = source[first : first + LANES, cols:]


def whole_kernel(info, o0, o1, o2, o3, out):
    for k, o in enumerate((o0, o1, o2, o3)):
        out[:, pl.ds(pl.multiple_of((info[0] ^ k) * TILE, TILE), TILE)] = o[...]


def mix_kernel(info, t0, t1, t2, t3, m0, m1, m2, m3, wo, hidden_ref, own_ref, scale_ref, mixed):
    place = info[0]
    for k, m in enumerate((m0, m1, m2, m3)):
        mixed[:, pl.ds(pl.multiple_of((place ^ k) * TILE, TILE), TILE)] = m[...]
    for k, t in enumerate((t0, t1, t2, t3)):
        rows = pl.ds(pl.multiple_of((place ^ k) * TILE, TILE), TILE)
        total = t[:TILE, :].astype(F32) + dot(mixed[rows, :], wo[...])
        scale = lax.rsqrt(jnp.mean(total * total, axis=1, keepdims=True) + EPS)
        hidden_ref[k * TILE : (k + 1) * TILE, :] = (total * scale).astype(BF16)
        if k == 0:
            own_ref[...] = total
            scale_ref[...] = jnp.broadcast_to(scale, scale_ref.shape)


def feed_kernel(hidden_ref, c0, c1, c2, c3, w_ref, act_ref, turned_ref, give, far, keep, w):
    units = w.shape[0] // 3
    for p in range(w_ref.shape[0]):
        width = w_ref.shape[2]
        w[:, p * width : (p + 1) * width] = w_ref[p]
    gw, uw, dw = (w[n * units : (n + 1) * units, :] for n in range(3))
    outs = ((keep, 0), (give, 0), (far, 0), (give, TILE))
    for k, c in enumerate((c0, c1, c2, c3)):
        at = slice(k * TILE, (k + 1) * TILE)
        h = hidden_ref[at, :]
        gate = dot(h, gw, NT)
        lift = dot(h, uw, NT)
        grad = dot(c[...], dw, NT)
        sig = 1.0 / (1.0 + jnp.exp(-gate))
        silu = gate * sig
        act = (silu * lift).astype(BF16)
        gate_back = (grad * lift * (sig + silu * (1.0 - sig))).astype(BF16)
        lift_back = (grad * silu).astype(BF16)
        act_ref[at, :] = act
        out, first = outs[k]
        out[first : first + TILE, :] = (dot(gate_back, gw) + dot(lift_back, uw)).astype(out.dtype)
        turned_ref[:units, at] = gate_back.T
        turned_ref[units : 2 * units, at] = lift_back.T
        turned_ref[2 * units :, at] = act.T


def feed(hidden, cots, weights):
    rows, model = hidden.shape
    units = weights.shape[1] // 3
    return call(
        feed_kernel,
        (
            shape(rows, units, BF16),
            shape(3 * units, rows, BF16),
            shape(rows // 2, model, BF16),
            shape(rows // 4, model, F32),
            shape(rows // 4, model, F32),
        ),
        (),
        (hidden, *cots, weights),
        [pltpu.VMEM((3 * units, model), BF16)], us=15)


def feed_grad_kernel(first, info, hidden, *refs):
    cots, (turned, give, keep, whole) = refs[:-4], refs[-4:]
    split = 2 * (turned.shape[0] // 3)
    last = first + give.shape[0]
    width = hidden.shape[1] // 8
    half = hidden.shape[1] // 2
    for start, end in ((first, min(last, split)), (max(first, split), last)):
        if start >= end:
            continue
        if start < split:
            total = dot(turned[start:end, :], hidden[...])
        else:
            total = sum(dot(turned[start:end, k * TILE : (k + 1) * TILE], c[...]) for k, c in enumerate(cots))
        out = slice(start - first, end - first)
        for p in range(8):
            spot = pl.ds(pl.multiple_of(info[8 + p] * width, width), width)
            whole[out, spot] = total[:, p * width : (p + 1) * width].astype(BF16)
    keep[...] = whole[:, :half]
    give[...] = whole[:, half:]


def feed_grad(info, first, rows, hidden, cots, turned, after=()):
    model = hidden.shape[1]
    return call(
        functools.partial(feed_grad_kernel, first),
        (shape(rows, model // 2, BF16),) * 2,
        (info,),
        (hidden, *cots, turned),
        [pltpu.VMEM((rows, model), BF16)],
        after=after,
    )


def middle_kernel(keep, got, own, *sends):
    size = own.shape[1]
    own[...] = keep[:, :size].astype(F32) + got[:, :size].astype(F32)
    for k in (1, 2, 3):
        cols = slice(k * size, (k + 1) * size)
        sends[k - 1][...] = (keep[:, cols].astype(F32) + got[:, cols].astype(F32)).astype(BF16)


def middle(give, keep, after=()):
    units, half = keep.shape
    if lax.axis_size("dp") != 8:
        whole = jnp.concatenate([keep, give], axis=1).astype(F32)
        return [lax.psum_scatter(whole, "dp", scatter_dimension=1, tiled=True)]
    outs = (shape(units, half // 4, F32),) + (shape(units, half // 4, BF16),) * 3
    own, *sends = call(middle_kernel, outs, (), (keep, swap(give, "dp", 1)), after=after)
    return [own] + [swap(sends[k - 1], "dp", 2 * k) for k in (1, 2, 3)]


def sum_kernel(*refs):
    total = refs[0][...]
    for t in refs[1:-1]:
        total = total + t[...].astype(F32)
    refs[-1][...] = total


def sum_terms(terms, after=()):
    if len(terms) == 1:
        return terms[0]
    return call(sum_kernel, shape(*terms[0].shape, F32), (), tuple(terms), after=after)


def after_kernel(keep, first, got, after_ref, scale_ref, cot, grad_ref, low_ref):
    total = keep[...] + first[:TILE, :].astype(F32) + got[...].astype(F32)
    after = after_ref[...]
    scale = scale_ref[:, :1]
    inner = jnp.mean(after * total, axis=1, keepdims=True)
    grad = cot[...].astype(F32) + scale * total - after * (scale * scale * scale * inner)
    grad_ref[...] = grad
    low_ref[...] = grad.astype(BF16)


def tokens_kernel(info, keep, first, got, scale_ref, tokens, grad, out, straight):
    for p in range(8):
        spot = pl.ds(pl.multiple_of(info[8 + p] * LANES, LANES), LANES)
        straight[:, p * LANES : (p + 1) * LANES] = keep[:, spot] + first[:TILE, spot].astype(F32) + got[:, spot].astype(F32)
    total = straight[...]
    x = tokens[:TILE, :].astype(F32)
    scale = scale_ref[pl.ds(pl.multiple_of(info[0] * TILE, TILE), TILE), :][:, :1]
    out[...] = grad[...] + total - x * (scale * scale * jnp.mean(x * total, axis=1, keepdims=True))


def result_kernel(act, w_ref, give, far, keep):
    units = act.shape[1]
    width = w_ref.shape[2]
    for k, (out, first) in enumerate(((keep, 0), (give, 0), (far, 0), (give, TILE))):
        a = act[k * TILE : (k + 1) * TILE, :]
        for p in range(0, w_ref.shape[0], 2):
            w = jnp.concatenate([w_ref[p, 2 * units :, :], w_ref[p + 1, 2 * units :, :]], axis=1)
            out[first : first + TILE, p * width : (p + 2) * width] = dot(a, w).astype(out.dtype)


def pack_kernel(info, wq, wk, wv, wo, wg, wu, wd, mixer, feed, *outs):
    place = info[0]
    scaled = lambda w, gain: (w[...].astype(F32) * gain[...]).astype(BF16)
    arrays = [scaled(w, mixer) for w in (wq, wk, wv)] + [wo[...]] + [scaled(w, feed) for w in (wg, wu)] + [wd[...]]
    for k, out in enumerate(outs):
        member = place ^ k
        first = 0
        for a in arrays:
            width = a.shape[1] // 4
            best = a[:, :width]
            for q in (1, 2, 3):
                best = jnp.where(member == q, a[:, q * width : (q + 1) * width], best)
            out[:, first : first + width] = best
            first += width


def cut_kernel(first, turn, info, p0, p1, p2, p3, out, whole):
    rows, width = p0.shape[0], whole.shape[1]
    for k, p in enumerate((p0, p1, p2, p3)):
        at = pl.ds(pl.multiple_of((info[0] ^ k) * rows, rows), rows)
        whole[at, :] = p[:, first : first + width].astype(F32)
    a = whole[...]
    out[...] = (a.T if turn else a).astype(BF16)


def cut(info, pieces, first, width, turn, after=(), us=2):
    rows = 4 * pieces[0].shape[0]
    if lax.axis_size("dp") != 8:
        a = in_order(pieces, info[0])[:, first : first + width]
        return a.T if turn else a
    out = shape(width, rows, BF16) if turn else shape(rows, width, BF16)
    return call(
        functools.partial(cut_kernel, first, turn), out, (info,), tuple(pieces), [pltpu.VMEM((rows, width), F32)], after=after, us=us, spare=7 * SPARE
    )


def pack_tokens_kernel(tokens, live, out):
    height = tokens.shape[0]
    out[:height, :] = tokens[...]
    out[height:, :] = jnp.broadcast_to(live[...], out[height:, :].shape).astype(BF16)


def copy_kernel(a, out):
    out[...] = a[...]


def finish_kernel(info, summed, own, t1, t2, t3, e0, e1, e2, e3, turned, whole):
    rows = e0.shape[0] // 3
    chunk = own.shape[0]
    total = own[...]
    for t in (t1, t2, t3):
        total = total + t[...].astype(F32)
    turned[:chunk, :] = total
    turned[chunk:, :] = summed[...]
    units = turned.shape[0] // 3
    for n in range(3):
        whole[...] = turned[n * units : (n + 1) * units, :].T
        for k, out in enumerate((e0, e1, e2, e3)):
            there = pl.ds(pl.multiple_of((info[0] ^ k) * rows, rows), rows)
            out[n * rows : (n + 1) * rows, :] = whole[there, :].astype(BF16)


def finish(info, place, summed, terms, after=()):
    height, rows = summed.shape[0] + terms[0].shape[0], summed.shape[1]
    units = height // 3
    if len(terms) == 1:
        both = jnp.concatenate([terms[0], summed], axis=0)
        blocks = [blocks_of(both[n * units : (n + 1) * units].T.astype(BF16), place) for n in range(3)]
        return [jnp.concatenate([b[k] for b in blocks], axis=0) for k in range(4)]
    return call(
        finish_kernel,
        (shape(3 * rows // 4, units, BF16),) * 4,
        (info,),
        (summed, *terms),
        [pltpu.VMEM((height, rows), F32), pltpu.VMEM((rows, units), F32)],
        after=after,
    )


def far_kernel(far, got, out):
    out[...] = (far[...] + got[out.shape[0] :, :].astype(F32)).astype(BF16)


def output_kernel(after, keep, first, got, out):
    out[...] = after[...] + keep[...] + first[: out.shape[0], :].astype(F32) + got[...].astype(F32)


def inputs_kernel(info, back, wa, wb, give, far, keep):
    half = wa.shape[0]
    for k, (out, first) in enumerate(((keep, 0), (give, 0), (far, 0), (give, TILE))):
        a = back[pl.ds(pl.multiple_of((info[0] ^ k) * TILE, TILE), TILE), :]
        out[first : first + TILE, :half] = dot(a, wa[:, : a.shape[1]], NT).astype(out.dtype)
        out[first : first + TILE, half:] = dot(a, wb[:, : a.shape[1]], NT).astype(out.dtype)


def late_middle_kernel(x, back, other, got, own, s1, s2, s3):
    half, width = got.shape[0], back.shape[1]
    rows = half // 4
    one = dot(x[:, :half], back[...], TN) + got[:, :width].astype(F32)
    two = other[...].astype(F32) + got[:, width:].astype(F32)
    own[:, :width] = one[:rows]
    own[:, width:] = two[:rows]
    for k, out in ((1, s1), (2, s2), (3, s3)):
        out[:, :width] = one[k * rows : (k + 1) * rows].astype(BF16)
        out[:, width:] = two[k * rows : (k + 1) * rows].astype(BF16)


def late_middle(x, back, other, give, after):
    half, cols = x.shape[1] // 2, back.shape[1] + other.shape[1]
    if lax.axis_size("dp") != 8:
        keep = jnp.concatenate([dot(x[:, :half], back, TN), other.astype(F32)], axis=1)
        whole = jnp.concatenate([keep, give.astype(F32)], axis=0)
        return [lax.psum_scatter(whole, "dp", scatter_dimension=0, tiled=True)]
    own, *sends = call(
        late_middle_kernel,
        (shape(half // 4, cols, F32),) + (shape(half // 4, cols, BF16),) * 3,
        (),
        (x, back, other, swap(give, "dp", 1)),
        after=after,
    )
    return [own] + [swap(sends[k - 1], "dp", 2 * k) for k in (1, 2, 3)]


def body(
    tokens,
    offsets,
    live_tokens,
    gain_mixer,
    query_weight,
    key_weight,
    value_weight,
    output_weight,
    gain_feed,
    gate_weight,
    up_weight,
    down_weight,
    cotangent,
):
    team = lax.axis_size("fsdp")
    place = lax.axis_index("fsdp")
    height, model = tokens.shape
    length = height * team
    units = gate_weight.shape[1] // team
    kq, kv, ko = (w.shape[1] // team for w in (query_weight, value_weight, output_weight))
    width = 2 * kq + kv
    own_rows = gain_mixer.shape[0]
    slots, blocks = layout()
    info = jnp.concatenate([jnp.full((8,), place, jnp.int32), slots, blocks])

    mixer_col = gain_mixer.astype(F32)[:, None]
    feed_col = gain_feed.astype(F32)[:, None]
    packs = call(
        pack_kernel,
        (shape(own_rows, width + ko + 3 * units, BF16),) * 4,
        (info,),
        (query_weight, key_weight, value_weight, output_weight, gate_weight, up_weight, down_weight, mixer_col, feed_col),
        spare=7 * SPARE,
    )
    packs = exchange(packs)
    first = cut(info, packs, 0, width + ko, False, us=2)
    wa, wb = gather(first, 0)
    feed_w = lax.all_gather(cut(info, packs, width + ko, 3 * units, True, after=(first,), us=2), "dp", axis=0)
    live_row = jnp.pad(live_tokens.astype(F32)[None, :], ((0, 0), (0, model - height)))
    packed = team_pieces(
        call(pack_tokens_kernel, shape(height + 16, model, BF16), (), (tokens, live_row), after=tuple(packs[1:]), us=2)
    )
    straight = call(functools.partial(straight_kernel, width), shape(model, ko, BF16), (info,), (wa, wb), us=2)
    xp, raw, mixed, exact, den, scale_one, row = attend(info, offsets, packed, wa, wb, width, after=(straight,))
    outs = team_pieces(straight)
    wo = call(whole_kernel, shape(model, model, BF16), (info,), tuple(outs), us=3)

    mixes = team_pieces(mixed)
    cots = team_pieces(call(copy_kernel, shape(height, model, BF16), (), (cotangent,), after=(packed[2],)))
    hidden, after, scale_two = call(
        mix_kernel,
        (shape(length, model, BF16), shape(height, model, F32), shape(height, LANES, F32)),
        (info,),
        (*packed, *mixes, wo),
        [pltpu.VMEM((length, model), BF16)], us=7)

    act, turned, give, far, keep = feed(hidden, cots, feed_w)
    got = swap(give, "fsdp", 1)
    far = call(far_kernel, shape(height, model, BF16), (), (far, got))
    chunk = SPLIT
    give_b, keep_b = feed_grad(info, chunk, 3 * units - chunk, hidden, cots, turned, after=(far,))
    give_a, keep_a = feed_grad(info, 0, chunk, hidden, (), turned, after=(give_b,))
    grad_after, low = call(
        after_kernel,
        (shape(height, model, F32), shape(height, model, BF16)),
        (),
        (keep, got, swap(far, "fsdp", 2), after, scale_two, cotangent),
        after=(give_a,),
    )
    grads = team_pieces(low)

    terms_b = middle(give_b, keep_b, after=(low,))

    qkv_back, give_l, out_part = attend_back(info, offsets, raw, grads, wo, exact, den, row, scale_one, xp, mixes, after=(terms_b[0],))

    sum_b = sum_terms(terms_b, after=(qkv_back,))
    terms_a = middle(give_a, keep_a, after=(sum_b,))
    give1, far1, keep1 = call(
        inputs_kernel,
        (shape(2 * height, model, BF16), shape(height, model, F32), shape(height, model, F32)),
        (info,),
        (qkv_back, wa, wb),
        after=(terms_a[0],),
    )
    got1 = swap(give1, "fsdp", 1)
    far1 = call(far_kernel, shape(height, model, BF16), (), (far1, got1))
    give2, far2, keep2 = call(
        result_kernel,
        (shape(2 * height, model, BF16), shape(height, model, F32), shape(height, model, F32)),
        (),
        (act, feed_w),
        after=(far1,),
    )
    got2 = swap(give2, "fsdp", 1)
    far2 = call(far_kernel, shape(height, model, BF16), (), (far2, got2))
    far_got2 = swap(far2, "fsdp", 2)
    terms_l = late_middle(xp, qkv_back, out_part, give_l, after=(far2,))
    tokens_grad = call(
        tokens_kernel,
        shape(height, model, F32),
        (info,),
        (keep1, got1, swap(far1, "fsdp", 2), scale_one, packed[0], grad_after),
        [pltpu.VMEM((height, model), F32)],
        after=(terms_l[0],),
    )
    output = call(
        output_kernel,
        shape(height, model, F32),
        (),
        (after, keep2, got2, far_got2),
        after=(tokens_grad,),
    )
    feed_pieces = finish(info, place, sum_b, terms_a, (output,))
    def spread(pieces):
        near = jnp.where(place % 2 == 0, jnp.stack(pieces[:2]), jnp.stack(pieces[1::-1]))
        away = jnp.where(place % 2 == 0, jnp.stack(pieces[2:]), jnp.stack(pieces[:1:-1]))
        whole = jnp.where(place // 2 == 0, jnp.concatenate([near, away], 0), jnp.concatenate([away, near], 0))
        return lambda r, a, b: jnp.concatenate([whole[k, r : r + own_rows, a:b] for k in range(team)], axis=1).astype(F32)

    over = lambda w, g: jnp.sum(w.astype(F32) * g, axis=1)
    wide = spread(exchange(feed_pieces))
    gate_sum, up_sum, down_grad = wide(0, 0, units), wide(own_rows, 0, units), wide(2 * own_rows, 0, units)
    gain_feed_grad = over(gate_weight, gate_sum) + over(up_weight, up_sum)
    gate_grad, up_grad = gate_sum * feed_col, up_sum * feed_col
    late = sum_terms(terms_l, after=(gain_feed_grad, gate_grad, up_grad, down_grad))
    late = spread(exchange(blocks_of(late.astype(BF16), place)))
    q_sum, k_sum, v_sum = late(0, 0, kq), late(0, kq, 2 * kq), late(0, 2 * kq, width)
    out_grad = late(0, width, width + ko)
    gain_mixer_grad = over(query_weight, q_sum) + over(key_weight, k_sum) + over(value_weight, v_sum)
    return (
        output,
        tokens_grad,
        gain_mixer_grad,
        q_sum * mixer_col,
        k_sum * mixer_col,
        v_sum * mixer_col,
        out_grad,
        gain_feed_grad,
        gate_grad,
        up_grad,
        down_grad,
    )


def solution(mesh):
    rows = P(("dp", "fsdp"), None)
    flat = P(("dp", "fsdp"))
    return jax.shard_map(
        body,
        mesh=mesh,
        in_specs=(rows, P("dp", None), flat, flat, rows, rows, rows, rows, flat, rows, rows, rows, rows),
        out_specs=(rows, rows, flat, rows, rows, rows, rows, flat, rows, rows, rows),
        check_vma=False,
    )
```

```python
import functools
import math

import jax
import jax.numpy as jnp
from jax import lax
from jax.experimental import pallas as pl
from jax.experimental.pallas import tpu as pltpu
from jax.sharding import PartitionSpec as P

FDIM = 16
VDIM = 64
EPS = 1e-05
TILE = 256
LANES = 128
SPARE = 8 * 1024 * 1024
SPLIT = 1024

F32 = jnp.float32
BF16 = jnp.bfloat16
NT = ((1,), (1,))
TN = ((0,), (0,))


def dot(a, b, dims=((1,), (0,))):
    return lax.dot_general(a, b, (dims, ((), ())), preferred_element_type=F32)


def shape(rows, cols, dtype):
    return jax.ShapeDtypeStruct((rows, cols), dtype)


def padded(dims, dtype):
    rows, cols = dims[-2:]
    return math.prod(dims[:-2]) * (rows + -rows % 16) * (cols + -cols % LANES) * jnp.dtype(dtype).itemsize


def call(kernel, outs, scalars, arrays, scratch=(), after=(), us=4, spare=SPARE):
    used = len(scalars) + len(arrays)

    def run(*refs):
        kernel(*refs[:used], *refs[used + len(after) :])

    smem = pl.BlockSpec(memory_space=pltpu.SMEM)
    vmem = pl.BlockSpec(memory_space=pltpu.VMEM)
    anywhere = pl.BlockSpec(memory_space=pl.ANY)
    held = sum(padded(a.shape, a.dtype) for a in (*arrays, *jax.tree.leaves(outs), *scratch))
    return pl.pallas_call(
        run,
        out_shape=outs,
        in_specs=[smem] * len(scalars) + [vmem] * len(arrays) + [anywhere] * len(after),
        out_specs=jax.tree.map(lambda _: vmem, outs),
        scratch_shapes=list(scratch),
        compiler_params=pltpu.CompilerParams(vmem_limit_bytes=held + spare),
        cost_estimate=pl.CostEstimate(flops=1, bytes_accessed=us * 3_000_000, transcendentals=0),
    )(*scalars, *arrays, *after)


def swap(a, axis, bit):
    n = lax.axis_size(axis)
    return lax.ppermute(a, axis, [(i, i ^ bit) for i in range(n)])


def part(a, start, size):
    return lax.dynamic_slice_in_dim(a, start, size, 0)


def pick(flag, one, two):
    return jnp.where(flag == 0, jnp.concatenate([one, two], 0), jnp.concatenate([two, one], 0))


def team_pieces(a):
    far = swap(a, "fsdp", 2)
    return a, swap(a, "fsdp", 1), far, swap(far, "fsdp", 1)


def blocks_of(a, place):
    rows = a.shape[0] // 4
    return [part(a, (place ^ k) * rows, rows) for k in range(4)]


def exchange(blocks):
    return [blocks[0]] + [swap(blocks[k], "fsdp", k) for k in (1, 2, 3)]


def in_order(pieces, place):
    high, low = place // 2, place % 2
    return pick(high, pick(low, pieces[0], pieces[1]), pick(low, pieces[2], pieces[3]))


def layout():
    block = jnp.arange(8, dtype=jnp.int32)
    if lax.axis_size("dp") != 8:
        return block, block
    at = lax.axis_index("dp")
    z, y = at // 2, at % 2
    return ((block % 2) ^ y) * 4 + ((block // 2) ^ z), 2 * ((block % 4) ^ z) + ((block // 4) ^ y)


def gather(a, axis):
    if lax.axis_size("dp") != 8:
        whole = lax.all_gather(a, "dp", axis=axis, tiled=True)
        half = whole.shape[axis] // 2
        return lax.slice_in_dim(whole, 0, half, axis=axis), lax.slice_in_dim(whole, half, 2 * half, axis=axis)
    mine = jnp.concatenate([a] + [swap(a, "dp", 2 * k) for k in (1, 2, 3)], axis)
    return mine, swap(mine, "dp", 1)


def lane_of(dims):
    return lax.broadcasted_iota(jnp.int32, dims, len(dims) - 1)


def query_cols(both):
    high = both.astype(BF16).astype(F32)
    low = both - high
    left = lane_of(both.shape) < 64
    one = jnp.where(left, high, pltpu.roll(low, 64, 1))
    two = jnp.where(left, high, 0.0)
    return jnp.concatenate([one.astype(BF16), two.astype(BF16)], axis=1)


def key_cols(both):
    high = both.astype(BF16).astype(F32)
    low = both - high
    left = lane_of(both.shape) < 64
    one = jnp.where(left, pltpu.roll(high, 64, 1), high)
    two = jnp.where(left, pltpu.roll(low, 64, 1), 0.0)
    return jnp.concatenate([one.astype(BF16), two.astype(BF16)], axis=1)


def head_only(a, h, width):
    lane = lane_of(a.shape)
    if width == FDIM:
        lane = lane % 64
    return jnp.where(lane // width == h, a, jnp.zeros_like(a))


def doc_starts(offsets_ref, i):
    place = i * TILE + lax.broadcasted_iota(jnp.int32, (TILE, 1), 0)
    start = jnp.zeros((TILE, 1), jnp.int32)
    for d in range(offsets_ref.shape[1]):
        first = offsets_ref[0, d]
        start = jnp.where(first <= place, jnp.maximum(start, first), start)
    return start


def allowed(start, row, i, j):
    ok = row >= start
    if i == j:
        place = i * TILE + lax.broadcasted_iota(jnp.int32, (TILE, TILE), 0)
        ok = ok & (row <= place)
    return ok


def forward_kernel(info, offsets_ref, t0, t1, t2, t3, wa, wb, xp, raw_ref, mixed_ref, exact_ref, den_ref, scale_ref, row_ref, qc, kc, vc):
    place = info[0]
    blocks = xp.shape[0] // TILE
    half = wa.shape[0]
    team_heads = vc.shape[1] // VDIM
    for k, t in enumerate((t0, t1, t2, t3)):
        block = place ^ k
        at = pl.ds(pl.multiple_of(block * TILE, TILE), TILE)
        x = t[:TILE, :]
        for p in range(8):
            xp[at, pl.ds(pl.multiple_of(info[8 + p] * LANES, LANES), LANES)] = x[:, p * LANES : (p + 1) * LANES]
        live = t[TILE : TILE + 16, :TILE].astype(F32)[:1, :]
        place_row = block * TILE + lane_of((1, TILE))
        row_ref[block] = jnp.broadcast_to(jnp.where(live > 0.5, place_row, -1), (8, TILE))
    for i in range(blocks):
        at = pl.ds(i * TILE, TILE)
        x = xp[at, :]
        wide = x.astype(F32)
        scale = lax.rsqrt(jnp.mean(wide * wide, axis=1, keepdims=True) + EPS)
        scale_ref[at, :] = jnp.broadcast_to(scale, (TILE, LANES))
        raw = (dot(x[:, :half], wa[:, : raw_ref.shape[1]]) + dot(x[:, half:], wb[:, : raw_ref.shape[1]])) * scale
        raw_ref[at, :] = raw
        both = raw[:, :LANES]
        qc[at, :] = query_cols(both)
        kc[at, :] = key_cols(both)
        vc[at, :] = raw[:, LANES:].astype(BF16)
    for i in range(blocks):
        at = pl.ds(i * TILE, TILE)
        start = doc_starts(offsets_ref, i)
        q = qc[at, :]
        result = jnp.zeros((TILE, vc.shape[1]), F32)
        dens = jnp.zeros((TILE, LANES), F32)
        for h in range(team_heads):
            total = jnp.zeros((TILE, vc.shape[1]), F32)
            den = jnp.zeros((TILE, 1), F32)
            qh = head_only(q, h, FDIM)
            for j in range(i + 1):
                there = pl.ds(j * TILE, TILE)
                s = dot(qh, kc[there, :], NT)
                kept = 1.0 + s * (0.25 + s * 0.03125)
                kept = jnp.where(allowed(start, row_ref[j][:1, :], i, j), kept, 0.0)
                den = den + jnp.sum(kept, axis=1, keepdims=True)
                total = total + dot(kept.astype(BF16), vc[there, :])
            result = jnp.where(lane_of(result.shape) // VDIM == h, total / den, result)
            dens = jnp.where(lane_of(dens.shape) == h, den, dens)
        exact_ref[at, :] = result
        mixed_ref[at, :] = result.astype(BF16)
        den_ref[at, :] = dens


def attend(info, offsets, tokens, wa, wb, width, after=()):
    length = 4 * TILE
    value = width - LANES
    model = tokens[0].shape[1]
    return call(
        forward_kernel,
        (
            shape(length, model, BF16),
            shape(length, width, F32),
            shape(length, value, BF16),
            shape(length, value, F32),
            shape(length, LANES, F32),
            shape(length, LANES, F32),
            jax.ShapeDtypeStruct((4, 8, TILE), jnp.int32),
        ),
        (info, offsets),
        (*tokens, wa, wb),
        [pltpu.VMEM((length, 256), BF16), pltpu.VMEM((length, 256), BF16), pltpu.VMEM((length, value), BF16)], after=after, us=9)


def backward_kernel(info, offsets_ref, raw_ref, g0, g1, g2, g3, wo, exact_ref, den_ref, row_ref, scale_ref, xp, m0, m1, m2, m3, back_ref, give_ref, keep_ref, gm, other, qc, kc, qr, kr, vc, acc, over):
    place = info[0]
    blocks = raw_ref.shape[0] // TILE
    team_heads = vc.shape[1] // VDIM
    mine_rows = pl.ds(pl.multiple_of(place * TILE, TILE), TILE)
    for k, g in enumerate((g0, g1, g2, g3)):
        at = pl.ds(pl.multiple_of((place ^ k) * TILE, TILE), TILE)
        gm[at, :] = dot(g[...], wo[mine_rows, :], NT)
    for i in range(blocks):
        at = pl.ds(i * TILE, TILE)
        raw = raw_ref[at, :]
        both = raw[:, :LANES]
        qc[at, :] = query_cols(both)
        kc[at, :] = key_cols(both)
        turned = pltpu.roll(both, 64, 1)
        left = lane_of(both.shape) < 64
        kr[at, :] = jnp.where(left, turned, 0.0).astype(BF16)
        qr[at, :] = jnp.where(left, 0.0, turned).astype(BF16)
        vc[at, :] = raw[:, LANES:].astype(BF16)
    acc[...] = jnp.zeros_like(acc)
    over[...] = jnp.zeros_like(over)
    for i in range(blocks):
        at = pl.ds(i * TILE, TILE)
        start = doc_starts(offsets_ref, i)
        q = qc[at, :]
        grad = gm[at, :]
        product = grad * exact_ref[at, :]
        dens = den_ref[at, :]
        heads = []
        for h in range(team_heads):
            inverse = 1.0 / jnp.sum(jnp.where(lane_of(dens.shape) == h, dens, 0.0), axis=1, keepdims=True)
            numer = head_only(grad * inverse, h, VDIM).astype(BF16)
            denom = -jnp.sum(head_only(product, h, VDIM), axis=1, keepdims=True) * inverse
            mine = qr[at, :].T[64 + h * FDIM : 64 + (h + 1) * FDIM, :]
            heads.append((head_only(q, h, FDIM), numer, denom, mine, numer.T[h * VDIM : (h + 1) * VDIM, :]))
        for j in range(i + 1):
            there = pl.ds(j * TILE, TILE)
            ok = allowed(start, row_ref[j][:1, :], i, j)
            keys = kc[there, :]
            values = vc[there, :]
            straight = kr[there, :]
            back = jnp.zeros((TILE, LANES), F32)
            for h, (qh, numer, denom, mine, tall) in enumerate(heads):
                s = dot(qh, keys, NT)
                kept = jnp.where(ok, 1.0 + s * (0.25 + s * 0.03125), 0.0)
                inner = dot(numer, values, NT) + denom
                inner = jnp.where(ok, inner * (0.25 + s * 0.0625), 0.0).astype(BF16)
                back = back + head_only(dot(inner, straight), h, FDIM)
                keys_rows = slice(64 + h * FDIM, 64 + (h + 1) * FDIM)
                value_rows = slice(LANES + h * VDIM, LANES + (h + 1) * VDIM)
                over[keys_rows, there] += dot(mine, inner)
                over[value_rows, there] += dot(tall, kept.astype(BF16))
            acc[at, :] += back
    for i in range(blocks):
        at = pl.ds(i * TILE, TILE)
        both = over[:, at].T
        scale = scale_ref[at, :1]
        back_ref[at, :LANES] = ((acc[at, :] + both[:, :LANES]) * scale).astype(BF16)
        back_ref[at, LANES:] = (both[:, LANES:] * scale).astype(BF16)
    mine = pl.ds(pl.multiple_of(place * TILE, TILE), TILE)
    for k, m in enumerate((m0, m1, m2, m3)):
        total = jnp.zeros((m.shape[1], TILE), F32)
        for b, g in enumerate((g0, g1, g2, g3)):
            rows = pl.ds(pl.multiple_of((place ^ b) * TILE, TILE), TILE)
            total = total + dot(m[rows, :], g[:, mine], TN)
        for side in (0, 1):
            spot = info[8 + 2 * (place ^ k) + side]
            other[pl.ds(pl.multiple_of(spot * LANES, LANES), LANES), :] = total[side * LANES : (side + 1) * LANES].astype(BF16)
    half, width = give_ref.shape[0], back_ref.shape[1]
    give_ref[:, :width] = dot(xp[:, half:], back_ref[...], TN).astype(BF16)
    give_ref[:, width:] = other[half:, :]
    keep_ref[...] = other[:half, :]


def attend_back(info, offsets, raw, grads, wo, exact, den, row, scale, xp, mixes, after=()):
    length, width = raw.shape
    model, cols = xp.shape[1], grads[0].shape[1] // 4
    value = width - LANES
    return call(
        backward_kernel,
        (
            shape(length, width, BF16),
            shape(model // 2, width + cols, BF16),
            shape(model // 2, cols, BF16),
        ),
        (info, offsets),
        (raw, *grads, wo, exact, den, row, scale, xp, *mixes),
        [
            pltpu.VMEM((length, value), F32),
            pltpu.VMEM((model, cols), BF16),
            pltpu.VMEM((length, 256), BF16),
            pltpu.VMEM((length, 256), BF16),
            pltpu.VMEM((length, LANES), BF16),
            pltpu.VMEM((length, LANES), BF16),
            pltpu.VMEM((length, value), BF16),
            pltpu.VMEM((length, LANES), F32),
            pltpu.VMEM((width, length), F32),
        ],
        after=after, us=18)


def straight_kernel(cols, info, a, b, out):
    for n in range(8):
        source, first = (a, n * LANES) if n < 4 else (b, (n - 4) * LANES)
        out[pl.ds(pl.multiple_of(info[16 + n] * LANES, LANES), LANES), :] = source[first : first + LANES, cols:]


def whole_kernel(info, o0, o1, o2, o3, out):
    for k, o in enumerate((o0, o1, o2, o3)):
        out[:, pl.ds(pl.multiple_of((info[0] ^ k) * TILE, TILE), TILE)] = o[...]


def mix_kernel(info, t0, t1, t2, t3, m0, m1, m2, m3, wo, hidden_ref, own_ref, scale_ref, mixed):
    place = info[0]
    for k, m in enumerate((m0, m1, m2, m3)):
        mixed[:, pl.ds(pl.multiple_of((place ^ k) * TILE, TILE), TILE)] = m[...]
    for k, t in enumerate((t0, t1, t2, t3)):
        rows = pl.ds(pl.multiple_of((place ^ k) * TILE, TILE), TILE)
        total = t[:TILE, :].astype(F32) + dot(mixed[rows, :], wo[...])
        scale = lax.rsqrt(jnp.mean(total * total, axis=1, keepdims=True) + EPS)
        hidden_ref[k * TILE : (k + 1) * TILE, :] = (total * scale).astype(BF16)
        if k == 0:
            own_ref[...] = total
            scale_ref[...] = jnp.broadcast_to(scale, scale_ref.shape)


def feed_kernel(hidden_ref, c0, c1, c2, c3, w_ref, act_ref, turned_ref, give, far, keep, w):
    units = w.shape[0] // 3
    for p in range(w_ref.shape[0]):
        width = w_ref.shape[2]
        w[:, p * width : (p + 1) * width] = w_ref[p]
    gw, uw, dw = (w[n * units : (n + 1) * units, :] for n in range(3))
    outs = ((keep, 0), (give, 0), (far, 0), (give, TILE))
    for k, c in enumerate((c0, c1, c2, c3)):
        at = slice(k * TILE, (k + 1) * TILE)
        h = hidden_ref[at, :]
        gate = dot(h, gw, NT)
        lift = dot(h, uw, NT)
        grad = dot(c[...], dw, NT)
        sig = 1.0 / (1.0 + jnp.exp(-gate))
        silu = gate * sig
        act = (silu * lift).astype(BF16)
        gate_back = (grad * lift * (sig + silu * (1.0 - sig))).astype(BF16)
        lift_back = (grad * silu).astype(BF16)
        act_ref[at, :] = act
        out, first = outs[k]
        out[first : first + TILE, :] = (dot(gate_back, gw) + dot(lift_back, uw)).astype(out.dtype)
        turned_ref[:units, at] = gate_back.T
        turned_ref[units : 2 * units, at] = lift_back.T
        turned_ref[2 * units :, at] = act.T


def feed(hidden, cots, weights):
    rows, model = hidden.shape
    units = weights.shape[1] // 3
    return call(
        feed_kernel,
        (
            shape(rows, units, BF16),
            shape(3 * units, rows, BF16),
            shape(rows // 2, model, BF16),
            shape(rows // 4, model, F32),
            shape(rows // 4, model, F32),
        ),
        (),
        (hidden, *cots, weights),
        [pltpu.VMEM((3 * units, model), BF16)], us=15)


def feed_grad_kernel(first, info, hidden, *refs):
    cots, (turned, give, keep, whole) = refs[:-4], refs[-4:]
    split = 2 * (turned.shape[0] // 3)
    last = first + give.shape[0]
    width = hidden.shape[1] // 8
    half = hidden.shape[1] // 2
    for start, end in ((first, min(last, split)), (max(first, split), last)):
        if start >= end:
            continue
        if start < split:
            total = dot(turned[start:end, :], hidden[...])
        else:
            total = sum(dot(turned[start:end, k * TILE : (k + 1) * TILE], c[...]) for k, c in enumerate(cots))
        out = slice(start - first, end - first)
        for p in range(8):
            spot = pl.ds(pl.multiple_of(info[8 + p] * width, width), width)
            whole[out, spot] = total[:, p * width : (p + 1) * width].astype(BF16)
    keep[...] = whole[:, :half]
    give[...] = whole[:, half:]


def feed_grad(info, first, rows, hidden, cots, turned, after=()):
    model = hidden.shape[1]
    return call(
        functools.partial(feed_grad_kernel, first),
        (shape(rows, model // 2, BF16),) * 2,
        (info,),
        (hidden, *cots, turned),
        [pltpu.VMEM((rows, model), BF16)],
        after=after,
    )


def middle_kernel(keep, got, own, *sends):
    size = own.shape[1]
    own[...] = keep[:, :size].astype(F32) + got[:, :size].astype(F32)
    for k in (1, 2, 3):
        cols = slice(k * size, (k + 1) * size)
        sends[k - 1][...] = (keep[:, cols].astype(F32) + got[:, cols].astype(F32)).astype(BF16)


def middle(give, keep, after=()):
    units, half = keep.shape
    if lax.axis_size("dp") != 8:
        whole = jnp.concatenate([keep, give], axis=1).astype(F32)
        return [lax.psum_scatter(whole, "dp", scatter_dimension=1, tiled=True)]
    outs = (shape(units, half // 4, F32),) + (shape(units, half // 4, BF16),) * 3
    own, *sends = call(middle_kernel, outs, (), (keep, swap(give, "dp", 1)), after=after)
    return [own] + [swap(sends[k - 1], "dp", 2 * k) for k in (1, 2, 3)]


def sum_kernel(*refs):
    total = refs[0][...]
    for t in refs[1:-1]:
        total = total + t[...].astype(F32)
    refs[-1][...] = total


def sum_terms(terms, after=()):
    if len(terms) == 1:
        return terms[0]
    return call(sum_kernel, shape(*terms[0].shape, F32), (), tuple(terms), after=after)


def after_kernel(keep, first, got, after_ref, scale_ref, cot, grad_ref, low_ref):
    total = keep[...] + first[:TILE, :].astype(F32) + got[...].astype(F32)
    after = after_ref[...]
    scale = scale_ref[:, :1]
    inner = jnp.mean(after * total, axis=1, keepdims=True)
    grad = cot[...].astype(F32) + scale * total - after * (scale * scale * scale * inner)
    grad_ref[...] = grad
    low_ref[...] = grad.astype(BF16)


def tokens_kernel(info, keep, first, got, scale_ref, tokens, grad, out, straight):
    for p in range(8):
        spot = pl.ds(pl.multiple_of(info[8 + p] * LANES, LANES), LANES)
        straight[:, p * LANES : (p + 1) * LANES] = keep[:, spot] + first[:TILE, spot].astype(F32) + got[:, spot].astype(F32)
    total = straight[...]
    x = tokens[:TILE, :].astype(F32)
    scale = scale_ref[pl.ds(pl.multiple_of(info[0] * TILE, TILE), TILE), :][:, :1]
    out[...] = grad[...] + total - x * (scale * scale * jnp.mean(x * total, axis=1, keepdims=True))


def result_kernel(act, w_ref, give, far, keep):
    units = act.shape[1]
    width = w_ref.shape[2]
    for k, (out, first) in enumerate(((keep, 0), (give, 0), (far, 0), (give, TILE))):
        a = act[k * TILE : (k + 1) * TILE, :]
        for p in range(0, w_ref.shape[0], 2):
            w = jnp.concatenate([w_ref[p, 2 * units :, :], w_ref[p + 1, 2 * units :, :]], axis=1)
            out[first : first + TILE, p * width : (p + 2) * width] = dot(a, w).astype(out.dtype)


def pack_kernel(info, wq, wk, wv, wo, wg, wu, wd, mixer, feed, *outs):
    place = info[0]
    scaled = lambda w, gain: (w[...].astype(F32) * gain[...]).astype(BF16)
    arrays = [scaled(w, mixer) for w in (wq, wk, wv)] + [wo[...]] + [scaled(w, feed) for w in (wg, wu)] + [wd[...]]
    for k, out in enumerate(outs):
        member = place ^ k
        first = 0
        for a in arrays:
            width = a.shape[1] // 4
            best = a[:, :width]
            for q in (1, 2, 3):
                best = jnp.where(member == q, a[:, q * width : (q + 1) * width], best)
            out[:, first : first + width] = best
            first += width


def cut_kernel(first, turn, info, p0, p1, p2, p3, out, whole):
    rows, width = p0.shape[0], whole.shape[1]
    for k, p in enumerate((p0, p1, p2, p3)):
        at = pl.ds(pl.multiple_of((info[0] ^ k) * rows, rows), rows)
        whole[at, :] = p[:, first : first + width].astype(F32)
    a = whole[...]
    out[...] = (a.T if turn else a).astype(BF16)


def cut(info, pieces, first, width, turn, after=(), us=2):
    rows = 4 * pieces[0].shape[0]
    if lax.axis_size("dp") != 8:
        a = in_order(pieces, info[0])[:, first : first + width]
        return a.T if turn else a
    out = shape(width, rows, BF16) if turn else shape(rows, width, BF16)
    return call(
        functools.partial(cut_kernel, first, turn), out, (info,), tuple(pieces), [pltpu.VMEM((rows, width), F32)], after=after, us=us, spare=7 * SPARE
    )


def pack_tokens_kernel(tokens, live, out):
    height = tokens.shape[0]
    out[:height, :] = tokens[...]
    out[height:, :] = jnp.broadcast_to(live[...], out[height:, :].shape).astype(BF16)


def copy_kernel(a, out):
    out[...] = a[...]


def finish_kernel(info, summed, own, t1, t2, t3, e0, e1, e2, e3, turned, whole):
    rows = e0.shape[0] // 3
    chunk = own.shape[0]
    total = own[...]
    for t in (t1, t2, t3):
        total = total + t[...].astype(F32)
    turned[:chunk, :] = total
    turned[chunk:, :] = summed[...]
    units = turned.shape[0] // 3
    for n in range(3):
        whole[...] = turned[n * units : (n + 1) * units, :].T
        for k, out in enumerate((e0, e1, e2, e3)):
            there = pl.ds(pl.multiple_of((info[0] ^ k) * rows, rows), rows)
            out[n * rows : (n + 1) * rows, :] = whole[there, :].astype(BF16)


def finish(info, place, summed, terms, after=()):
    height, rows = summed.shape[0] + terms[0].shape[0], summed.shape[1]
    units = height // 3
    if len(terms) == 1:
        both = jnp.concatenate([terms[0], summed], axis=0)
        blocks = [blocks_of(both[n * units : (n + 1) * units].T.astype(BF16), place) for n in range(3)]
        return [jnp.concatenate([b[k] for b in blocks], axis=0) for k in range(4)]
    return call(
        finish_kernel,
        (shape(3 * rows // 4, units, BF16),) * 4,
        (info,),
        (summed, *terms),
        [pltpu.VMEM((height, rows), F32), pltpu.VMEM((rows, units), F32)],
        after=after,
    )


def far_kernel(far, got, out):
    out[...] = (far[...] + got[out.shape[0] :, :].astype(F32)).astype(BF16)


def output_kernel(after, keep, first, got, out):
    out[...] = after[...] + keep[...] + first[: out.shape[0], :].astype(F32) + got[...].astype(F32)


def inputs_kernel(info, back, wa, wb, give, far, keep):
    half = wa.shape[0]
    for k, (out, first) in enumerate(((keep, 0), (give, 0), (far, 0), (give, TILE))):
        a = back[pl.ds(pl.multiple_of((info[0] ^ k) * TILE, TILE), TILE), :]
        out[first : first + TILE, :half] = dot(a, wa[:, : a.shape[1]], NT).astype(out.dtype)
        out[first : first + TILE, half:] = dot(a, wb[:, : a.shape[1]], NT).astype(out.dtype)


def late_middle_kernel(x, back, other, got, own, s1, s2, s3):
    half, width = got.shape[0], back.shape[1]
    rows = half // 4
    one = dot(x[:, :half], back[...], TN) + got[:, :width].astype(F32)
    two = other[...].astype(F32) + got[:, width:].astype(F32)
    own[:, :width] = one[:rows]
    own[:, width:] = two[:rows]
    for k, out in ((1, s1), (2, s2), (3, s3)):
        out[:, :width] = one[k * rows : (k + 1) * rows].astype(BF16)
        out[:, width:] = two[k * rows : (k + 1) * rows].astype(BF16)


def late_middle(x, back, other, give, after):
    half, cols = x.shape[1] // 2, back.shape[1] + other.shape[1]
    if lax.axis_size("dp") != 8:
        keep = jnp.concatenate([dot(x[:, :half], back, TN), other.astype(F32)], axis=1)
        whole = jnp.concatenate([keep, give.astype(F32)], axis=0)
        return [lax.psum_scatter(whole, "dp", scatter_dimension=0, tiled=True)]
    own, *sends = call(
        late_middle_kernel,
        (shape(half // 4, cols, F32),) + (shape(half // 4, cols, BF16),) * 3,
        (),
        (x, back, other, swap(give, "dp", 1)),
        after=after,
    )
    return [own] + [swap(sends[k - 1], "dp", 2 * k) for k in (1, 2, 3)]


def body(
    tokens,
    offsets,
    live_tokens,
    gain_mixer,
    query_weight,
    key_weight,
    value_weight,
    output_weight,
    gain_feed,
    gate_weight,
    up_weight,
    down_weight,
    cotangent,
):
    team = lax.axis_size("fsdp")
    place = lax.axis_index("fsdp")
    height, model = tokens.shape
    length = height * team
    units = gate_weight.shape[1] // team
    kq, kv, ko = (w.shape[1] // team for w in (query_weight, value_weight, output_weight))
    width = 2 * kq + kv
    own_rows = gain_mixer.shape[0]
    slots, blocks = layout()
    info = jnp.concatenate([jnp.full((8,), place, jnp.int32), slots, blocks])

    mixer_col = gain_mixer.astype(F32)[:, None]
    feed_col = gain_feed.astype(F32)[:, None]
    packs = call(
        pack_kernel,
        (shape(own_rows, width + ko + 3 * units, BF16),) * 4,
        (info,),
        (query_weight, key_weight, value_weight, output_weight, gate_weight, up_weight, down_weight, mixer_col, feed_col),
        spare=7 * SPARE,
    )
    packs = exchange(packs)
    first = cut(info, packs, 0, width + ko, False, us=2)
    wa, wb = gather(first, 0)
    feed_w = lax.all_gather(cut(info, packs, width + ko, 3 * units, True, after=(first,), us=2), "dp", axis=0)
    live_row = jnp.pad(live_tokens.astype(F32)[None, :], ((0, 0), (0, model - height)))
    packed = team_pieces(
        call(pack_tokens_kernel, shape(height + 16, model, BF16), (), (tokens, live_row), after=tuple(packs[1:]), us=2)
    )
    straight = call(functools.partial(straight_kernel, width), shape(model, ko, BF16), (info,), (wa, wb), us=2)
    xp, raw, mixed, exact, den, scale_one, row = attend(info, offsets, packed, wa, wb, width, after=(straight,))
    outs = team_pieces(straight)
    wo = call(whole_kernel, shape(model, model, BF16), (info,), tuple(outs), us=3)

    mixes = team_pieces(mixed)
    cots = team_pieces(call(copy_kernel, shape(height, model, BF16), (), (cotangent,), after=(packed[2],)))
    hidden, after, scale_two = call(
        mix_kernel,
        (shape(length, model, BF16), shape(height, model, F32), shape(height, LANES, F32)),
        (info,),
        (*packed, *mixes, wo),
        [pltpu.VMEM((length, model), BF16)], us=7)

    act, turned, give, far, keep = feed(hidden, cots, feed_w)
    got = swap(give, "fsdp", 1)
    far = call(far_kernel, shape(height, model, BF16), (), (far, got))
    chunk = SPLIT
    give_b, keep_b = feed_grad(info, chunk, 3 * units - chunk, hidden, cots, turned, after=(far,))
    give_a, keep_a = feed_grad(info, 0, chunk, hidden, (), turned, after=(give_b,))
    grad_after, low = call(
        after_kernel,
        (shape(height, model, F32), shape(height, model, BF16)),
        (),
        (keep, got, swap(far, "fsdp", 2), after, scale_two, cotangent),
        after=(give_a,),
    )
    grads = team_pieces(low)

    terms_b = middle(give_b, keep_b, after=(low,))

    qkv_back, give_l, out_part = attend_back(info, offsets, raw, grads, wo, exact, den, row, scale_one, xp, mixes, after=(terms_b[0],))

    terms_a = middle(give_a, keep_a, after=(qkv_back,))
    sum_b = sum_terms(terms_b, after=(terms_a[0],))
    give1, far1, keep1 = call(
        inputs_kernel,
        (shape(2 * height, model, BF16), shape(height, model, F32), shape(height, model, F32)),
        (info,),
        (qkv_back, wa, wb),
        after=(sum_b,),
    )
    got1 = swap(give1, "fsdp", 1)
    far1 = call(far_kernel, shape(height, model, BF16), (), (far1, got1))
    give2, far2, keep2 = call(
        result_kernel,
        (shape(2 * height, model, BF16), shape(height, model, F32), shape(height, model, F32)),
        (),
        (act, feed_w),
        after=(far1,),
    )
    got2 = swap(give2, "fsdp", 1)
    far2 = call(far_kernel, shape(height, model, BF16), (), (far2, got2))
    far_got2 = swap(far2, "fsdp", 2)
    terms_l = late_middle(xp, qkv_back, out_part, give_l, after=(far2,))
    tokens_grad = call(
        tokens_kernel,
        shape(height, model, F32),
        (info,),
        (keep1, got1, swap(far1, "fsdp", 2), scale_one, packed[0], grad_after),
        [pltpu.VMEM((height, model), F32)],
        after=(terms_l[0],),
    )
    output = call(
        output_kernel,
        shape(height, model, F32),
        (),
        (after, keep2, got2, far_got2),
        after=(tokens_grad,),
    )
    feed_pieces = finish(info, place, sum_b, terms_a, (output,))
    def spread(pieces):
        near = jnp.where(place % 2 == 0, jnp.stack(pieces[:2]), jnp.stack(pieces[1::-1]))
        away = jnp.where(place % 2 == 0, jnp.stack(pieces[2:]), jnp.stack(pieces[:1:-1]))
        whole = jnp.where(place // 2 == 0, jnp.concatenate([near, away], 0), jnp.concatenate([away, near], 0))
        return lambda r, a, b: jnp.concatenate([whole[k, r : r + own_rows, a:b] for k in range(team)], axis=1).astype(F32)

    over = lambda w, g: jnp.sum(w.astype(F32) * g, axis=1)
    wide = spread(exchange(feed_pieces))
    gate_sum, up_sum, down_grad = wide(0, 0, units), wide(own_rows, 0, units), wide(2 * own_rows, 0, units)
    gain_feed_grad = over(gate_weight, gate_sum) + over(up_weight, up_sum)
    gate_grad, up_grad = gate_sum * feed_col, up_sum * feed_col
    late = sum_terms(terms_l, after=(gain_feed_grad, gate_grad, up_grad, down_grad))
    late = spread(exchange(blocks_of(late.astype(BF16), place)))
    q_sum, k_sum, v_sum = late(0, 0, kq), late(0, kq, 2 * kq), late(0, 2 * kq, width)
    out_grad = late(0, width, width + ko)
    gain_mixer_grad = over(query_weight, q_sum) + over(key_weight, k_sum) + over(value_weight, v_sum)
    return (
        output,
        tokens_grad,
        gain_mixer_grad,
        q_sum * mixer_col,
        k_sum * mixer_col,
        v_sum * mixer_col,
        out_grad,
        gain_feed_grad,
        gate_grad,
        up_grad,
        down_grad,
    )


def solution(mesh):
    rows = P(("dp", "fsdp"), None)
    flat = P(("dp", "fsdp"))
    return jax.shard_map(
        body,
        mesh=mesh,
        in_specs=(rows, P("dp", None), flat, flat, rows, rows, rows, rows, flat, rows, rows, rows, rows),
        out_specs=(rows, rows, flat, rows, rows, rows, rows, flat, rows, rows, rows),
        check_vma=False,
    )
```
